256 devices in a mesh: grp: 32 (over y_lo, z, core), sub: 8 (over y_hi, x).
Axes of the slice: x: 4, y: 4 (y_hi: 2, y_lo: 2; y = y_hi * 2 + y_lo), z: 8, core: 2. Of those that a mesh axis runs over, the one named last changes fastest.
Arguments:
- state_zero: float32 [512, 16807], P(('grp', 'sub')), as said below
- state_one: float32 [256, 7776], P(('grp', 'sub')), as said below
- state_two: float32 [256, 7776], P(('grp', 'sub')), as said below
- state_three: float32 [256, 3125], P(('grp', 'sub')), as said below
- intra_zero: float32 [8, 7, 7], replicated, may hold values from -0.75 to 0.75
- intra_one: float32 [8, 6, 6], replicated, may hold values from -0.875 to 0.875
- intra_two: float32 [8, 6, 6], replicated, may hold values from -0.875 to 0.875
- intra_three: float32 [8, 5, 5], replicated, may hold values from -1 to 1
- intersections: float32 [3, 8, 7, 7], replicated, may hold values from -2 to 2
- positions: float32 [3, 8, 7, 7], replicated, may hold values from -2 to 2
- coupling_pair: int32 [24], replicated, may hold values from 0 to 2
- coupling_mode: int32 [24], replicated, may hold values from 0 to 7
- coupling_strength: float32 [24], replicated, may hold values from -3 to 3
Outputs:
- stepped_zero: float32 [512, 16807], P(('grp', 'sub'))
- stepped_one: float32 [256, 7776], P(('grp', 'sub'))
- stepped_two: float32 [256, 7776], P(('grp', 'sub'))
- stepped_three: float32 [256, 3125], P(('grp', 'sub'))
- density_zero: float32 [8, 7, 7], replicated
- density_one: float32 [8, 6, 6], replicated
- density_two: float32 [8, 6, 6], replicated
- density_three: float32 [8, 5, 5], replicated
The draws below stay inside these ranges and needn't reach their ends.
Inputs may be any that keep to these rules, and one draw needn't show every extreme that they name: `state_zero`: rows from 7**3 on are zero. `state_one`: rows from 6**3 on are zero. `state_two`: rows from 6**3 on are zero. `state_three`: rows from 5**3 on are zero.
All inputs are finite; a program needn't handle non-finite values.
Results may differ from the reference program's by a relative error of at most 0.0001.
Values sent between devices are 32-bit elements; how exact they have to be, the bound alone decides.
No kernel may reach another device: no remote copies, remote signals or barrier semaphores. Data moves between devices by JAX's collectives and lax.ppermute only.
A program may use at most 128 MiB of HBM per device.

```python
import math
import jax
import jax.numpy as jnp
from jax import lax

N0 = 7
N1 = 6
N2 = 6
N3 = 5
F = 8
PAIRS = 3
TERMS = 24
PAD0 = 512
PAD1 = 256
PAD2 = 256
PAD3 = 256


def state_draw(key, mode_width, rows_total):
    real_rows = mode_width ** 3
    columns = mode_width ** 5
    value_key, column_key = jax.random.split(key)
    row_pos = jnp.arange(rows_total).astype(jnp.float32)
    values = jax.random.normal(value_key, (rows_total, columns), jnp.float32)
    row_scale = 10.0 ** (row_pos / real_rows)
    divisor = 20.0
    live_rows = (row_pos < real_rows).astype(jnp.float32)
    tail_pos = (jnp.arange(columns) % real_rows).astype(jnp.float32)
    jitter = jax.random.uniform(column_key, (columns,), jnp.float32)
    column_scale = 10.0 ** (0.7 * tail_pos / real_rows + 0.3 * jitter)
    return values * (row_scale * live_rows)[:, None] * column_scale[None, :] / divisor


def draw_state_zero(key, part):
    return state_draw(jax.random.fold_in(key, 101), N0, PAD0)


def draw_state_one(key, part):
    return state_draw(jax.random.fold_in(key, 202), N1, PAD1)


def draw_state_two(key, part):
    return state_draw(jax.random.fold_in(key, 303), N2, PAD2)


def draw_state_three(key, part):
    return state_draw(jax.random.fold_in(key, 404), N3, PAD3)


def place_ends(entries, stream_key, low, largest):
    index_at = [jax.random.randint(jax.random.fold_in(stream_key, axis), (), 0, length) for axis, length in enumerate(entries.shape)]
    main_axis = entries.shape.index(max(entries.shape))
    neighbour = index_at[:main_axis] + [(index_at[main_axis] + 1) % entries.shape[main_axis]] + index_at[main_axis + 1:]
    return entries.at[tuple(index_at)].set(low).at[tuple(neighbour)].set(largest)


def scatter_about(own_key, extent, spread, limit, kind=jnp.bfloat16):
    entries = jax.random.normal(own_key, extent, jnp.float32) * spread
    return jnp.minimum(jnp.maximum(entries, -limit), limit).astype(kind)


def setup_inputs(seed: int = 0) -> dict:
    keys = jax.random.split(jax.random.key(seed), 14)
    return {
        "state_zero": draw_state_zero(jax.random.fold_in(keys[13], 71), 0),
        "state_one": draw_state_one(jax.random.fold_in(keys[13], 71), 0),
        "state_two": draw_state_two(jax.random.fold_in(keys[13], 71), 0),
        "state_three": draw_state_three(jax.random.fold_in(keys[13], 71), 0),
        "intra_zero": scatter_about(keys[4], (F, N0, N0), (F * N0) ** -0.5, 0.75, jnp.float32),
        "intra_one": scatter_about(keys[5], (F, N1, N1), (F * N1) ** -0.5, 0.875, jnp.float32),
        "intra_two": scatter_about(keys[6], (F, N2, N2), (F * N2) ** -0.5, 0.875, jnp.float32),
        "intra_three": scatter_about(keys[7], (F, N3, N3), (F * N3) ** -0.5, 1.0, jnp.float32),
        "intersections": scatter_about(keys[8], (PAIRS, F, N0, N0), N0 ** -0.5, 2.0, jnp.float32),
        "positions": scatter_about(keys[9], (PAIRS, F, N0, N0), N0 ** -0.5, 2.0, jnp.float32),
        "coupling_pair": place_ends(jax.random.randint(keys[10], (TERMS,), 0, PAIRS), jax.random.fold_in(keys[10], 1), 0, PAIRS - 1).astype(jnp.int32),
        "coupling_mode": place_ends(jax.random.randint(keys[11], (TERMS,), 0, F), jax.random.fold_in(keys[11], 1), 0, F - 1).astype(jnp.int32),
        "coupling_strength": scatter_about(keys[12], (TERMS,), 0.5, 3.0, jnp.float32),
    }


highest = lax.Precision.HIGHEST
time_step = 0.25


def along_mode(tensor, matrix, axis_at):
    old_shape = tensor.shape
    before = math.prod(old_shape[:axis_at])
    behind = math.prod(old_shape[axis_at + 1:])
    shaped = tensor.reshape(before, old_shape[axis_at], behind)
    result = jnp.einsum("ab,xby->xay", matrix, shaped, precision=highest)
    return result.reshape(old_shape[:axis_at] + (matrix.shape[0],) + old_shape[axis_at + 1:])


def coupled(source, over_mats, pos_mats, weights):
    zero_part = source
    one_part = None
    modes_count = source.ndim
    for axis_at in range(modes_count):
        moved_part = weights[axis_at] * along_mode(zero_part, pos_mats[axis_at], axis_at)
        if one_part is not None:
            moved_part = along_mode(one_part, over_mats[axis_at], axis_at) + moved_part
        if axis_at + 1 < modes_count:
            zero_part = along_mode(zero_part, over_mats[axis_at], axis_at)
        one_part = moved_part
    return one_part


def intra(tensor, operator_set):
    summed = jnp.zeros_like(tensor)
    for axis_at in range(tensor.ndim):
        summed = summed + along_mode(tensor, operator_set[axis_at], axis_at)
    return summed


def density(tensor):
    mode_width = tensor.shape[0]
    per_mode = []
    for axis_at in range(tensor.ndim):
        before = mode_width ** axis_at
        behind = mode_width ** (tensor.ndim - 1 - axis_at)
        shaped = tensor.reshape(before, mode_width, behind)
        per_mode.append(jnp.einsum("xiy,xjy->ij", shaped, shaped, precision=highest))
    return jnp.stack(per_mode) / float(mode_width ** (tensor.ndim - 1))


def reference(state_zero, state_one, state_two, state_three, intra_zero, intra_one, intra_two, intra_three, intersections, positions, coupling_pair, coupling_mode, coupling_strength):
    packed = [state_zero, state_one, state_two, state_three]
    operators = [intra_zero, intra_one, intra_two, intra_three]
    padded_rows = [PAD0, PAD1, PAD2, PAD3]
    widths = [N0, N1, N2, N3]
    tensors = []
    for state_index in range(4):
        span_rows = widths[state_index] ** 3
        tensors.append(packed[state_index][:span_rows].reshape((widths[state_index],) * F))
    pair_pick = (coupling_pair[:, None] == jnp.arange(PAIRS, dtype=jnp.int32)[None, :]).astype(coupling_strength.dtype)
    mode_pick = (coupling_mode[:, None] == jnp.arange(F, dtype=jnp.int32)[None, :]).astype(coupling_strength.dtype)
    weight_table = jnp.einsum("t,tp,tk->pk", coupling_strength, pair_pick, mode_pick, precision=highest)
    actions = [intra(tensors[state_index], operators[state_index]) for state_index in range(4)]
    for pair_index in range(PAIRS):
        lower_state = pair_index
        upper_state = pair_index + 1
        over_mats = intersections[pair_index, :, :widths[lower_state], :widths[upper_state]]
        pos_mats = positions[pair_index, :, :widths[lower_state], :widths[upper_state]]
        actions[lower_state] = actions[lower_state] + coupled(tensors[upper_state], over_mats, pos_mats, weight_table[pair_index])
        actions[upper_state] = actions[upper_state] + coupled(tensors[lower_state], jnp.transpose(over_mats, (0, 2, 1)), jnp.transpose(pos_mats, (0, 2, 1)), weight_table[pair_index])
    outputs = []
    densities = []
    for state_index in range(4):
        mode_width = widths[state_index]
        stepped = (tensors[state_index] - time_step * actions[state_index]).reshape(mode_width ** 3, mode_width ** (F - 3))
        filler = jnp.zeros((padded_rows[state_index] - mode_width ** 3, mode_width ** (F - 3)), stepped.dtype)
        outputs.append(jnp.concatenate([stepped, filler], axis=0))
        densities.append(density(tensors[state_index]))
    return (outputs[0], outputs[1], outputs[2], outputs[3], densities[0], densities[1], densities[2], densities[3])
```

```python
import functools

import jax
import jax.numpy as jnp
import numpy as np
from jax import lax
from jax.experimental import pallas as pl
from jax.experimental.pallas import tpu as pltpu
from jax.sharding import PartitionSpec as P

time_step = 0.25
axes = ("grp", "sub")
bf16 = jnp.bfloat16
f32 = jnp.float32
widths = (7, 6, 6, 5)
vmem_limit = 56 * 1024 * 1024

list_at = {"e": (0, 256), "o": (256, 256), "r1": (512, 256), "r3": (768, 256), "b0": (1024, 384)}
list_at["b1"] = list_at["r1"]
list_at["b3"] = (768, 128)
list_rows = 1408
lane_kinds = {"p7": 0, "p6": 1, "p5": 2, "t7": 3, "t6": 4, "t5": 5}


def digit_tables():
    row_digits = np.full((list_rows, 3), -1)

    def fill(start, values, width):
        for place, value in enumerate(values):
            if 0 <= value < width**3:
                row_digits[start + place] = (value // width**2, value // width % width, value % width)

    fill(0, [2 * place for place in range(256)], 7)
    fill(256, [2 * place + 1 for place in range(256)], 7)
    fill(512, list(range(256)), 6)
    fill(768, list(range(256)), 5)
    fill(1024, list(range(384)), 7)
    lane_digits = np.full((768, 2), -1)
    for kind, at in lane_kinds.items():
        width = int(kind[1])
        for lane in range(128):
            value = lane % 64 if kind[0] == "p" else lane
            if value < width**2:
                lane_digits[128 * at + lane] = (value // width, value % width)

    def one_hot(digits):
        return (digits[:, :, None] == np.arange(8)).astype(np.float32).transpose(1, 0, 2)

    def rest(digits, invalid):
        total = np.full((digits.shape[0], 8), float(invalid), np.float32)
        for slot in range(digits.shape[1]):
            value = np.zeros(digits.shape[0])
            for other in range(digits.shape[1]):
                if other != slot:
                    value = value * 8 + digits[:, other]
            total[:, slot] = np.where(digits[:, 0] < 0, invalid, value)
        return total

    row_one = np.tile(one_hot(row_digits), (1, 1, 3))
    lane_one = np.tile(one_hot(lane_digits), (1, 1, 3))
    return (
        row_one,
        np.ascontiguousarray(row_one.transpose(0, 2, 1)),
        rest(row_digits, -1),
        np.ascontiguousarray(rest(row_digits, -2).T),
        lane_one,
        np.ascontiguousarray(lane_one.transpose(0, 2, 1)),
        rest(lane_digits, -1),
        np.ascontiguousarray(rest(lane_digits, -2).T),
    )


def mm(left, right):
    return jnp.dot(left, right, preferred_element_type=f32)


def mm_nt(left, right):
    return lax.dot_general(left, right, (((1,), (1,)), ((), ())), preferred_element_type=f32)


def split(value):
    high = value.astype(bf16)
    return high, (value - high.astype(f32)).astype(bf16)


def mm3(left, right):
    return mm(left[0], right[0]) + mm(left[0], right[1]) + mm(left[1], right[0])


def mm3_nt(left, right):
    return mm_nt(left[0], right[0]) + mm_nt(left[0], right[1]) + mm_nt(left[1], right[0])


def put_matrix(mats, at, value):
    rows, columns = value.shape
    high = value.astype(bf16).astype(f32)
    middle = (value - high).astype(bf16).astype(f32)
    mats[at] = jnp.zeros((24, 8), f32)
    mats[at, 0:rows, 0:columns] = high
    mats[at, 8 : 8 + rows, 0:columns] = middle
    mats[at, 16 : 16 + rows, 0:columns] = value - high - middle


def get_matrix(mats, at):
    return mats[at].astype(bf16)


def expand(row_one, slot, rows, matrix, col_one, col_slot, cols, flipped):
    if flipped:
        left = mm_nt(row_one[slot, pl.ds(*rows), 0:8].astype(bf16), matrix).astype(bf16)
        return mm(left, col_one[col_slot, :, pl.ds(*cols)].astype(bf16))
    right = mm(matrix, col_one[col_slot, 0:8, pl.ds(*cols)].astype(bf16)).astype(bf16)
    return mm(row_one[slot, pl.ds(*rows), :].astype(bf16), right)


def fill_weights(pair_ref, mode_ref, strength_ref, weights):
    for at in range(24):
        weights[at] = 0.0
    for term in range(24):
        at = pair_ref[term] * 8 + mode_ref[term]
        weights[at] = weights[at] + strength_ref[term]


def fill_coupling(mats, over_ref, pos_ref, weights, modes):
    for pair in range(3):
        for mode in modes:
            put_matrix(mats, pair * 16 + mode, over_ref[pair, mode])
            put_matrix(mats, pair * 16 + 8 + mode, weights[pair * 8 + mode] * pos_ref[pair, mode])


def kron_three(tables, mats, pair, modes, rows, cols, flipped):
    row_one, col_one = tables[0], tables[1]

    def factor(slot, extra):
        matrix = get_matrix(mats, pair * 16 + extra + modes[slot])
        return expand(row_one, slot, rows, matrix, col_one, slot, cols, flipped)

    over_tail, over_mid = factor(2, 0), factor(1, 0)
    tail = over_mid * over_tail
    moved = factor(1, 8) * over_tail + over_mid * factor(2, 8)
    over_lead = factor(0, 0)
    return over_lead * tail, factor(0, 8) * tail + over_lead * moved


def sum_three(tables, mats, at, rows, cols):
    row_one, col_one, row_rest, col_rest = tables
    total = None
    for slot in range(3):
        part = expand(row_one, slot, rows, get_matrix(mats, at + slot), col_one, slot, cols, False)
        same = row_rest[pl.ds(*rows), slot : slot + 1] == col_rest[slot : slot + 1, pl.ds(*cols)]
        part = jnp.where(same, part, 0.0)
        total = part if total is None else total + part
    return total


def store_split(high_ref, low_ref, rows, cols, value):
    high, low = split(value)
    high_ref[pl.ds(*rows), pl.ds(*cols)] = high
    low_ref[pl.ds(*rows), pl.ds(*cols)] = low


def pack_kernel(zero_ref, one_ref, two_ref, three_ref, send_ref, own_ref, items):
    items[...] = jnp.zeros((256, 256), f32)
    for lead in range(49):
        for row in range(2):
            start = 343 * lead
            at = 128 * row
            items[at + lead : at + lead + 1, 0:256] = zero_ref[row : row + 1, start : start + 256]
            place, half = (lead, 0) if lead < 25 else (lead - 25, 128)
            items[at + 49 + place : at + 50 + place, half : half + 87] = zero_ref[
                row : row + 1, start + 256 : start + 343
            ]
    for lead in range(36):
        start = 216 * lead
        items[74 + lead : 75 + lead, 0:216] = one_ref[0:1, start : start + 216]
        items[202 + lead : 203 + lead, 0:216] = two_ref[0:1, start : start + 216]
    for lead in range(25):
        start = 125 * lead
        place, half = (lead, 0) if lead < 13 else (lead - 13, 128)
        items[238 + place : 239 + place, half : half + 125] = three_ref[0:1, start : start + 125]
    turned = items[...].T
    own_ref[...] = turned
    send_ref[:, 0, :] = turned


def lanes_of(shape):
    return lax.broadcasted_iota(jnp.int32, shape, 1)


def keep(value, low, high):
    lane = lanes_of(value.shape)
    return jnp.where((lane >= low) & (lane < high), value, 0.0)


def moved_to(value, source, target, count):
    shift = (target - source) % 128
    if shift:
        value = pltpu.roll(value, shift, 1)
    return keep(value, target, target + count)


def wide_from_items(value, source, target):
    head = moved_to(value, source, target, 49)
    tail = moved_to(value[0:128], source + 49, target, 25) + moved_to(
        value[128:256], source + 49, target + 25, 24
    )
    return jnp.concatenate([head, tail], axis=0)


def items_from_wide(value):
    head = keep(value[0:256], 0, 49)
    tail = value[256:384]
    low = moved_to(tail, 0, 49, 25)
    high = moved_to(tail, 25, 49, 24)
    return head + jnp.concatenate([low, high], axis=0)


def narrow_from_items(value, source, target):
    return moved_to(value[0:128], source, target, 13) + moved_to(
        value[128:256], source, target + 13, 12
    )


def items_from_narrow(value):
    return jnp.concatenate([moved_to(value, 0, 110, 13), moved_to(value, 13, 110, 12)], axis=0)


def own_views(own_ref):
    left, right = own_ref[:, 0:128], own_ref[:, 128:256]
    return (
        wide_from_items(left, 0, 0),
        wide_from_items(right, 0, 0),
        moved_to(left, 74, 0, 36),
        moved_to(right, 74, 0, 36),
        narrow_from_items(right, 110, 0),
    )


def put_density(dens_ref, mode, state, value):
    dens_ref[pl.ds((mode // 4) * 8, 8), pl.ds((mode % 4) * 32 + state * 8, 8)] = value


def collapse(gram, same, rows_one, cols_one):
    high, low = split(jnp.where(same, gram, 0.0))
    part = mm(cols_one, high) + mm(cols_one, low)
    part_high, part_low = split(part)
    return mm(part_high, rows_one) + mm(part_low, rows_one)


def lead_kernel(
    row_one,
    col_one,
    row_rest,
    col_rest,
    pair_ref,
    mode_ref,
    strength_ref,
    over_ref,
    pos_ref,
    intra_zero,
    intra_one,
    intra_two,
    intra_three,
    la_high,
    la_low,
    lb_high,
    lb_low,
    lc_high,
    lc_low,
    ld_high,
    ld_low,
    mats,
    weights,
):
    tables = (row_one, col_one, row_rest, col_rest)
    fill_weights(pair_ref, mode_ref, strength_ref, weights)
    fill_coupling(mats, over_ref, pos_ref, weights, range(3))
    for state, ref in enumerate((intra_zero, intra_one, intra_two, intra_three)):
        for mode in range(3):
            put_matrix(mats, 48 + 8 * state + mode, ref[mode])
    la = functools.partial(store_split, la_high, la_low)
    lb = functools.partial(store_split, lb_high, lb_low)
    lc = functools.partial(store_split, lc_high, lc_low)
    ld = functools.partial(store_split, ld_high, ld_low)
    even, odd, one, three = (list_at[name] for name in ("e", "o", "r1", "r3"))

    def kron(pair, rows, cols, flipped):
        return kron_three(tables, mats, pair, (0, 1, 2), rows, cols, flipped)

    def tile(store, row, col, value):
        store((256 * row, 256), (256 * col, 256), value)

    for col, source in enumerate((even, odd)):
        zero_part, one_part = kron(0, one, source, True)
        tile(la, 0, col, zero_part)
        tile(la, 1, col, one_part)
    zero_part, one_part = kron(2, three, one, True)
    tile(la, 0, 2, zero_part)
    tile(la, 1, 2, one_part)
    zero_part, one_part = kron(2, one, three, False)
    tile(la, 0, 3, zero_part)
    tile(la, 1, 3, one_part)
    tile(la, 2, 0, sum_three(tables, mats, 48, odd, even))
    tile(la, 2, 1, sum_three(tables, mats, 48, odd, odd))
    tile(la, 2, 2, sum_three(tables, mats, 64, one, one))
    tile(la, 2, 3, sum_three(tables, mats, 72, three, three))
    tile(lb, 0, 0, sum_three(tables, mats, 48, even, even))
    tile(lb, 0, 1, sum_three(tables, mats, 48, even, odd))
    tile(lb, 0, 2, sum_three(tables, mats, 56, one, one))
    zero_part, one_part = kron(0, even, one, False)
    tile(lc, 0, 0, zero_part)
    tile(lc, 0, 1, one_part)
    zero_part, one_part = kron(0, odd, one, False)
    tile(lc, 0, 2, zero_part)
    tile(lc, 1, 2, one_part)
    zero_part, one_part = kron(1, one, one, True)
    tile(lc, 1, 0, zero_part)
    tile(lc, 1, 1, one_part)
    zero_part, one_part = kron(1, one, one, False)
    tile(ld, 0, 0, zero_part)
    tile(ld, 0, 1, one_part)


def row_density_kernel(
    row_one, col_one, row_rest, col_rest, lane_one, lcol_one, lane_rest, lcol_rest, own_ref, dens_ref
):
    dens_ref[...] = jnp.zeros((16, 128), f32)
    views = own_views(own_ref)
    groups = (
        (0, jnp.concatenate([views[0], views[1]], axis=1), "b0", "t7"),
        (1, views[2], "b1", "t6"),
        (2, views[3], "b1", "t6"),
        (3, views[4], "b3", "t5"),
    )
    for state, view, index, kind in groups:
        parts = split(view)
        gram = mm3_nt(parts, parts)
        at = list_at[index]
        for slot in range(3):
            same = row_rest[pl.ds(*at), slot : slot + 1] == col_rest[slot : slot + 1, pl.ds(*at)]
            put_density(
                dens_ref,
                5 + slot,
                state,
                collapse(
                    gram,
                    same,
                    row_one[slot, pl.ds(*at), 0:8].astype(bf16),
                    col_one[slot, 0:8, pl.ds(*at)].astype(bf16),
                ),
            )
        if state == 0:
            turned = jnp.concatenate([views[0].T, views[1].T], axis=1)
        else:
            turned = view.T
        parts = split(turned)
        gram = mm3_nt(parts, parts)
        at = (128 * lane_kinds[kind], 128)
        for slot in range(2):
            same = lane_rest[pl.ds(*at), slot : slot + 1] == lcol_rest[slot : slot + 1, pl.ds(*at)]
            put_density(
                dens_ref,
                3 + slot,
                state,
                collapse(
                    gram,
                    same,
                    lane_one[slot, pl.ds(*at), 0:8].astype(bf16),
                    lcol_one[slot, 0:8, pl.ds(*at)].astype(bf16),
                ),
            )


def received_blocks(recv_ref):
    return recv_ref[:, 0, 0:128], recv_ref[:, 0, 128:256]


def middle_kernel(
    recv_ref, la_high, la_low, lb_high, lb_low, lc_high, lc_low, ld_high, ld_low, send_ref
):
    left, right = received_blocks(recv_ref)
    even, odd = split(keep(left, 0, 74)), split(keep(right, 0, 74))
    one_at = [split(moved_to(left, 74, target, 36)) for target in (74, 0, 36, 72)]
    two_at = [split(moved_to(right, 74, target, 36)) for target in (74, 0, 36)]
    three = split(keep(right, 110, 123))

    def product(high_ref, low_ref, stack):
        high = jnp.concatenate([part[0] for part in stack], axis=0)
        low = jnp.concatenate([part[1] for part in stack], axis=0)
        return mm3((high_ref[...], low_ref[...]), (high, low))

    value = product(la_high, la_low, [even, odd, two_at[0], three])
    send_ref[:, 0, 0:128] = value[0:256]
    send_ref[:, 0, 128:256] = value[256:512]
    send_ref[:, 0, 384:512] = value[512:768]
    send_ref[:, 0, 256:384] = product(lb_high, lb_low, [even, odd, one_at[0]])
    value = product(lc_high, lc_low, one_at[1:])
    send_ref[:, 0, 512:640] = value[0:256]
    send_ref[:, 0, 640:768] = value[256:512]
    send_ref[:, 0, 768:896] = product(ld_high, ld_low, two_at[1:])


def col_density_kernel(row_one, col_one, row_rest, col_rest, recv_ref, partial_ref, dens_ref):
    dens_ref[...] = partial_ref[...]
    left, right = received_blocks(recv_ref)
    even, odd = split(keep(left, 0, 74)), split(keep(right, 0, 74))
    groups = (
        (0, ((even, "e"), (odd, "o"))),
        (1, ((split(keep(left, 74, 110)), "r1"),)),
        (2, ((split(keep(right, 74, 110)), "r1"),)),
        (3, ((split(keep(right, 110, 123)), "r3"),)),
    )
    for state, members in groups:
        totals = [None, None, None]
        for first, first_name in members:
            for second, second_name in members:
                gram = mm3_nt(first, second)
                rows, cols = list_at[first_name], list_at[second_name]
                for slot in range(3):
                    same = (
                        row_rest[pl.ds(*rows), slot : slot + 1]
                        == col_rest[slot : slot + 1, pl.ds(*cols)]
                    )
                    value = collapse(
                        gram,
                        same,
                        row_one[slot, pl.ds(*cols), 0:8].astype(bf16),
                        col_one[slot, 0:8, pl.ds(*rows)].astype(bf16),
                    )
                    totals[slot] = value if totals[slot] is None else totals[slot] + value
        for slot in range(3):
            put_density(dens_ref, slot, state, totals[slot])


directions = (
    (0, False, "b0", "b1", "p6", "t7"),
    (0, True, "b1", "b0", "p7", "t6"),
    (1, False, "b1", "b1", "p6", "t6"),
    (1, True, "b1", "b1", "p6", "t6"),
    (2, False, "b1", "b3", "p5", "t6"),
    (2, True, "b3", "b1", "p6", "t5"),
)


def tail_kernel(
    row_one,
    col_one,
    row_rest,
    col_rest,
    lane_one,
    lcol_one,
    lane_rest,
    lcol_rest,
    pair_ref,
    mode_ref,
    strength_ref,
    over_ref,
    pos_ref,
    intra_zero,
    intra_one,
    intra_two,
    intra_three,
    own_ref,
    order_ref,
    *rest,
):
    tails, (home_ref, mats, weights) = rest[:24], rest[24:]
    tables = (row_one, col_one, row_rest, col_rest)
    fill_weights(pair_ref, mode_ref, strength_ref, weights)
    fill_coupling(mats, over_ref, pos_ref, weights, range(3, 8))
    for state, ref in enumerate((intra_zero, intra_one, intra_two, intra_three)):
        for mode in range(3, 8):
            put_matrix(mats, 48 + 8 * state + mode, ref[mode])
    row = lax.broadcasted_iota(jnp.int32, (128, 128), 0)
    for at, (pair, flipped, target, source, from_lanes, to_lanes) in enumerate(directions):
        three_high, three_low, two_high, two_low = tails[4 * at : 4 * at + 4]
        rows, cols = list_at[target], list_at[source]
        over, moved = kron_three(tables, mats, pair, (5, 6, 7), rows, cols, flipped)
        store_split(three_high, three_low, (0, rows[1]), (0, cols[1]), over)
        store_split(three_high, three_low, (rows[1], rows[1]), (0, cols[1]), moved)
        lanes_in = (128 * lane_kinds[from_lanes], 128)
        lanes_out = (128 * lane_kinds[to_lanes], 128)

        def factor(slot, extra):
            matrix = get_matrix(mats, pair * 16 + extra + 3 + slot)
            return expand(
                lane_one, slot, lanes_in, matrix, lcol_one, slot, lanes_out, not flipped
            )

        first, second = factor(0, 0), factor(1, 0)
        over = first * second
        moved = factor(0, 8) * second + first * factor(1, 8)
        store_split(two_high, two_low, (0, 128), (0, 128), jnp.where(row < 64, moved, over))
        store_split(two_high, two_low, (128, 128), (0, 128), jnp.where(row < 64, over, 0.0))
    views = own_views(own_ref)
    start = 0
    for view, state, index, kind in (
        (views[0], 0, "b0", "t7"),
        (views[1], 0, "b0", "t7"),
        (views[2], 1, "b1", "t6"),
        (views[3], 2, "b1", "t6"),
        (views[4], 3, "b3", "t5"),
    ):
        at = list_at[index]
        lanes = (128 * lane_kinds[kind], 128)
        three = split(sum_three(tables, mats, 48 + 8 * state + 5, at, at))
        two = None
        for slot in range(2):
            matrix = get_matrix(mats, 48 + 8 * state + 3 + slot)
            part = expand(lane_one, slot, lanes, matrix, lcol_one, slot, lanes, True)
            same = (
                lane_rest[pl.ds(*lanes), slot : slot + 1]
                == lcol_rest[slot : slot + 1, pl.ds(*lanes)]
            )
            part = jnp.where(same, part, 0.0)
            two = part if two is None else two + part
        parts = split(view)
        home_ref[pl.ds(start, at[1]), :] = mm3(three, parts) + mm3(parts, split(two))
        start += at[1]


def last_kernel(back_ref, own_ref, home_ref, *rest):
    tails, (zero_ref, one_ref, two_ref, three_ref, items) = rest[:24], rest[24:]

    def block(at):
        return back_ref[:, 0, 128 * at : 128 * at + 128]

    first, second, fifth, sixth, seventh = block(0), block(1), block(4), block(5), block(6)
    even_in = moved_to(fifth, 0, 0, 36) + moved_to(fifth, 36, 64, 36)
    odd_in = moved_to(fifth, 72, 0, 36) + moved_to(sixth, 72, 64, 36)
    inputs = (
        jnp.concatenate([even_in, odd_in], axis=1),
        wide_from_items(first, 0, 0) + wide_from_items(second, 0, 64),
        moved_to(seventh, 0, 0, 36) + moved_to(seventh, 36, 64, 36),
        moved_to(sixth, 0, 0, 36) + moved_to(sixth, 36, 64, 36),
        narrow_from_items(first, 110, 0) + narrow_from_items(second, 110, 64),
        moved_to(first, 74, 0, 36) + moved_to(second, 74, 64, 36),
    )
    sums = {}
    targets = (("e", "o"), ("one",), ("one",), ("two",), ("two",), ("three",))
    for at, value in enumerate(inputs):
        three_high, three_low, two_high, two_low = tails[4 * at : 4 * at + 4]
        height = three_high.shape[0] // 2
        middle = mm3((three_high[...], three_low[...]), split(value))
        for which, name in enumerate(targets[at]):
            lanes = slice(128 * which, 128 * which + 128)
            both = jnp.concatenate([middle[0:height, lanes], middle[height:, lanes]], axis=1)
            part = mm3(split(both), (two_high[...], two_low[...]))
            sums[name] = part if name not in sums else sums[name] + part
    start = 0
    for name, height in (("e", 384), ("o", 384), ("one", 256), ("two", 256), ("three", 128)):
        sums[name] = sums[name] + home_ref[pl.ds(start, height), :]
        start += height
    left = items_from_wide(sums["e"]) + moved_to(sums["one"], 0, 74, 36) + block(2)
    right = (
        items_from_wide(sums["o"])
        + moved_to(sums["two"], 0, 74, 36)
        + items_from_narrow(sums["three"])
        + block(3)
    )
    items[0:128, :] = (own_ref[:, 0:128] - time_step * left).T
    items[128:256, :] = (own_ref[:, 128:256] - time_step * right).T
    for lead in range(49):
        for row in range(2):
            start = 343 * lead
            at = 128 * row
            zero_ref[row : row + 1, start : start + 256] = items[at + lead : at + lead + 1, 0:256]
            place, half = (lead, 0) if lead < 25 else (lead - 25, 128)
            zero_ref[row : row + 1, start + 256 : start + 343] = items[
                at + 49 + place : at + 50 + place, half : half + 87
            ]
    for lead in range(36):
        start = 216 * lead
        one_ref[0:1, start : start + 216] = items[74 + lead : 75 + lead, 0:216]
        two_ref[0:1, start : start + 216] = items[202 + lead : 203 + lead, 0:216]
    for lead in range(25):
        start = 125 * lead
        place, half = (lead, 0) if lead < 13 else (lead - 13, 128)
        three_ref[0:1, start : start + 125] = items[238 + place : 239 + place, half : half + 125]


def density_kernel(dens_ref, zero_ref, one_ref, two_ref, three_ref):
    for state, ref in enumerate((zero_ref, one_ref, two_ref, three_ref)):
        width = widths[state]
        value = dens_ref[...] * (1.0 / float(width**7))
        for mode in range(8):
            row, lane = (mode // 4) * 8, (mode % 4) * 32 + state * 8
            ref[mode] = value[row : row + width, lane : lane + width]


def local(*args):
    states = args[:4]
    intra = args[4:8]
    over, pos, pair, mode, strength = args[8:]
    tables = [jnp.asarray(table) for table in digit_tables()]
    row_tables, lane_tables = tables[:4], tables[4:]
    vm = pl.BlockSpec(memory_space=pltpu.VMEM)
    sm = pl.BlockSpec(memory_space=pltpu.SMEM)

    def call(kernel, operands, outs, scratch=(), specs=None):
        return pl.pallas_call(
            kernel,
            out_shape=[jax.ShapeDtypeStruct(shape, kind) for shape, kind in outs],
            in_specs=specs or [vm] * len(operands),
            out_specs=[vm] * len(outs),
            scratch_shapes=list(scratch),
            compiler_params=pltpu.CompilerParams(vmem_limit_bytes=vmem_limit),
        )(*operands)

    def exchange(value):
        return lax.all_to_all(value, axes, split_axis=0, concat_axis=0, tiled=True)

    with jax.named_scope("pack"):
        send, own = call(
            pack_kernel,
            states,
            [((256, 1, 256), f32), ((256, 256), f32)],
            [pltpu.VMEM((256, 256), f32)],
        )
    with jax.named_scope("forward"):
        recv = exchange(send)
    mats = [pltpu.VMEM((80, 24, 8), f32), pltpu.SMEM((24,), f32)]
    with jax.named_scope("lead_matrices"):
        lead_outs = []
        for shape in ((768, 1024), (256, 768), (512, 768), (256, 512)):
            lead_outs += [(shape, bf16)] * 2
        lead = call(
            lead_kernel,
            [*row_tables, pair, mode, strength, over, pos, *intra],
            lead_outs,
            mats,
            [vm] * 4 + [sm] * 3 + [vm] * 6,
        )
    with jax.named_scope("row_density"):
        (partial,) = call(
            row_density_kernel, [*row_tables, *lane_tables, own], [((16, 128), f32)]
        )
    with jax.named_scope("lead_products"):
        (outgoing,) = call(middle_kernel, [recv, *lead], [((256, 1, 896), f32)])
    with jax.named_scope("back"):
        back = exchange(outgoing)
    with jax.named_scope("col_density"):
        (dens,) = call(col_density_kernel, [*row_tables, recv, partial], [((16, 128), f32)])
    with jax.named_scope("tail_matrices"):
        tail_outs = []
        for pair_at, flipped, target, source, from_lanes, to_lanes in directions:
            tail_outs += [((2 * list_at[target][1], list_at[source][1]), bf16)] * 2
            tail_outs += [((256, 128), bf16)] * 2
        tails = call(
            tail_kernel,
            [*row_tables, *lane_tables, pair, mode, strength, over, pos, *intra, own, dens],
            tail_outs + [((1408, 128), f32)],
            mats,
            [vm] * 8 + [sm] * 3 + [vm] * 8,
        )
        tails, home = tails[:-1], tails[-1]
    with jax.named_scope("density_sum"):
        for axis, size in (("grp", 32), ("sub", 8)):
            for bit in range(size.bit_length() - 1):
                swap = [(at, at ^ (1 << bit)) for at in range(size)]
                dens = dens + lax.ppermute(dens, axis, swap)
        densities = call(
            density_kernel,
            [dens],
            [((8, width, width), f32) for width in widths],
        )
    with jax.named_scope("tail_products"):
        stepped = call(
            last_kernel,
            [back, own, home, *tails],
            [(state.shape, f32) for state in states],
            [pltpu.VMEM((256, 256), f32)],
        )
    return (*stepped, *densities)


def solution(mesh):
    rows = P(axes, None)
    in_specs = (rows,) * 4 + (P(),) * 9
    out_specs = (rows,) * 4 + (P(),) * 4
    return jax.shard_map(local, mesh=mesh, in_specs=in_specs, out_specs=out_specs, check_vma=False)
```

```python
import functools
import itertools

import jax
import jax.numpy as jnp
import numpy as np
from jax import lax
from jax.experimental import pallas as pl
from jax.experimental.pallas import tpu as pltpu
from jax.sharding import PartitionSpec as P

time_step = 0.25
axes = ("grp", "sub")
bf16 = jnp.bfloat16
f32 = jnp.float32
vmem_limit = 56 * 1024 * 1024
widths = (7, 6, 6, 5)

list_at = {"e": (0, 256), "o": (256, 256), "r1": (512, 256), "r3": (768, 256), "b0": (1024, 384)}
list_at["b1"] = list_at["r1"]
list_at["b3"] = (768, 128)
list_rows = 1408
lane_kinds = {"p7": 0, "p6": 1, "p5": 2, "t7": 3, "t6": 4, "t5": 5}


def digit_tables():
    row_digits = np.full((list_rows, 3), -1)

    def fill(start, values, width):
        for place, value in enumerate(values):
            if 0 <= value < width**3:
                row_digits[start + place] = (value // width**2, value // width % width, value % width)

    fill(0, [2 * place for place in range(256)], 7)
    fill(256, [2 * place + 1 for place in range(256)], 7)
    fill(512, list(range(256)), 6)
    fill(768, list(range(256)), 5)
    fill(1024, list(range(384)), 7)
    lane_digits = np.full((768, 2), -1)
    for kind, at in lane_kinds.items():
        width = int(kind[1])
        for lane in range(128):
            value = lane % 64 if kind[0] == "p" else lane
            if value < width**2:
                lane_digits[128 * at + lane] = (value // width, value % width)

    def table(digits, invalid):
        total = np.full((digits.shape[0], 8), float(invalid), np.float32)
        valid = digits[:, 0] >= 0
        for slot in range(digits.shape[1]):
            value = np.zeros(digits.shape[0])
            for other in range(digits.shape[1]):
                if other != slot:
                    value = value * 8 + digits[:, other]
            total[:, slot] = np.where(valid, digits[:, slot], invalid)
            total[:, 3 + slot] = np.where(valid, value, invalid)
        return total

    return (
        table(row_digits, -1),
        np.ascontiguousarray(table(row_digits, -2).T),
        table(lane_digits, -1),
        np.ascontiguousarray(table(lane_digits, -2).T),
    )


class Lists:
    def __init__(self, row_ref, col_ref):
        self.row_ref, self.col_ref, self.made = row_ref, col_ref, {}

    def once(self, key, make):
        if key not in self.made:
            self.made[key] = make()
        return self.made[key]

    def rows_hot(self, slot, rows):
        def make():
            lane = lax.broadcasted_iota(jnp.int32, (rows[1], 24), 1) & 7
            digit = self.row_ref[pl.ds(*rows), slot : slot + 1]
            return jnp.where(digit == lane.astype(f32), 1.0, 0.0).astype(bf16)

        return self.once(("r", slot, rows), make)

    def cols_hot(self, slot, cols):
        def make():
            place = lax.broadcasted_iota(jnp.int32, (8, cols[1]), 0)
            digit = self.col_ref[slot : slot + 1, pl.ds(*cols)]
            return jnp.where(digit == place.astype(f32), 1.0, 0.0).astype(bf16)

        return self.once(("c", slot, cols), make)

    def same(self, slot, rows, cols):
        left = self.row_ref[pl.ds(*rows), 3 + slot : 4 + slot]
        return left == self.col_ref[3 + slot : 4 + slot, pl.ds(*cols)]


def mm(left, right):
    return jnp.dot(left, right, preferred_element_type=f32)


def mm_nt(left, right):
    return lax.dot_general(left, right, (((1,), (1,)), ((), ())), preferred_element_type=f32)


def split(value):
    high = value.astype(bf16)
    return high, (value - high.astype(f32)).astype(bf16)


def mm3(left, right):
    return mm(left[0], right[0]) + mm(left[0], right[1]) + mm(left[1], right[0])


def mm3_nt(left, right):
    return mm_nt(left[0], right[0]) + mm_nt(left[0], right[1]) + mm_nt(left[1], right[0])


def put_matrix(mats, at, value):
    rows, columns = value.shape
    high = value.astype(bf16).astype(f32)
    middle = (value - high).astype(bf16).astype(f32)
    mats[at] = jnp.zeros((24, 8), f32)
    mats[at, 0:rows, 0:columns] = high
    mats[at, 8 : 8 + rows, 0:columns] = middle
    mats[at, 16 : 16 + rows, 0:columns] = value - high - middle


def expand(lists, slot, rows, matrix, cols):
    right = mm(matrix.astype(bf16), lists.cols_hot(slot, cols)).astype(bf16)
    return mm(lists.rows_hot(slot, rows), right)


def fill_weights(pair_ref, mode_ref, strength_ref, weights):
    for at in range(24):
        weights[at] = 0.0
    for term in range(24):
        at = pair_ref[term] * 8 + mode_ref[term]
        weights[at] = weights[at] + strength_ref[term]


mats_count = 128


def fill_coupling(mats, over_ref, pos_ref, weights, wanted):
    for pair, flipped, modes in wanted:
        for mode in modes:
            over = over_ref[pair, :, mode, :]
            moved = weights[pair * 8 + mode] * pos_ref[pair, :, mode, :]
            at = pair * 32 + mode
            if flipped:
                over, moved, at = over.T, moved.T, at + 16
            put_matrix(mats, at, over)
            put_matrix(mats, at + 8, moved)


def fill_operators(mats, refs, modes):
    for state, ref in enumerate(refs):
        for mode in modes:
            put_matrix(mats, 96 + 8 * state + mode, ref[:, mode, :])


def kron_three(lists, mats, pair, modes, rows, cols, flipped):
    base = pair * 32 + (16 if flipped else 0)

    def factor(slot, extra):
        return expand(lists, slot, rows, mats[base + extra + modes[slot]], cols)

    over_tail, over_mid = factor(2, 0), factor(1, 0)
    tail = over_mid * over_tail
    moved = factor(1, 8) * over_tail + over_mid * factor(2, 8)
    over_lead = factor(0, 0)
    return over_lead * tail, factor(0, 8) * tail + over_lead * moved


def sum_slots(lists, mats, at, slots, rows, cols, turned=False):
    total = None
    for slot in range(slots):
        matrix = mats[at + slot]
        part = expand(lists, slot, rows, matrix, cols)
        part = jnp.where(lists.same(slot, rows, cols), part, 0.0)
        total = part if total is None else total + part
    return total


def store_split(high_ref, low_ref, rows, cols, value):
    high, low = split(value)
    high_ref[pl.ds(*rows), pl.ds(*cols)] = high
    low_ref[pl.ds(*rows), pl.ds(*cols)] = low


def lanes_of(shape):
    return lax.broadcasted_iota(jnp.int32, shape, 1)


def keep(value, low, high):
    lane = lanes_of(value.shape)
    return jnp.where((lane >= low) & (lane < high), value, 0.0)


def moved_to(value, source, target, count):
    shift = (target - source) % 128
    if shift:
        value = pltpu.roll(value, shift, 1)
    return keep(value, target, target + count)


def wide_from_items(value, source, target):
    head = moved_to(value, source, target, 49)
    tail = moved_to(value[0:128], source + 49, target, 25) + moved_to(
        value[128:256], source + 49, target + 25, 24
    )
    return jnp.concatenate([head, tail], axis=0)


def items_from_wide(value):
    head = keep(value[0:256], 0, 49)
    tail = value[256:384]
    low = moved_to(tail, 0, 49, 25)
    high = moved_to(tail, 25, 49, 24)
    return head + jnp.concatenate([low, high], axis=0)


def narrow_from_items(value, source, target):
    return moved_to(value[0:128], source, target, 13) + moved_to(
        value[128:256], source, target + 13, 12
    )


def items_from_narrow(value):
    return jnp.concatenate([moved_to(value, 0, 110, 13), moved_to(value, 13, 110, 12)], axis=0)


def own_views(own_ref):
    left, right = own_ref[:, 0:128], own_ref[:, 128:256]
    return (
        wide_from_items(left, 0, 0),
        wide_from_items(right, 0, 0),
        moved_to(left, 74, 0, 36),
        moved_to(right, 74, 0, 36),
        narrow_from_items(right, 110, 0),
    )


row_units = (
    [((1, 2), mode) for mode in (5, 6, 7)]
    + [((0,), mode) for mode in (5, 6, 7)]
    + [((3,), mode) for mode in (5, 6, 7)]
    + [((state,), mode) for state in range(4) for mode in (3, 4)]
)
col_units = [(states, mode) for states in ((1, 2), (0,), (3,)) for mode in (0, 1, 2)]


def density_tables():
    def entries(units, second):
        listed = []
        for unit, (states, mode) in enumerate(units):
            for half, state in enumerate(states):
                width = widths[state]
                for low in range(width):
                    for high in range(low, width):
                        shift = high - low
                        place = shift * 8 + low if shift <= 4 else (8 - shift) * 8 + high
                        listed.append((second * half + 40 * unit + place, state, mode, low, high))
        return listed

    pick = np.zeros((512, 256), np.float32)
    rows = np.zeros((64, 2, 1280), np.float32)
    cols = np.zeros((2, 1280, 128), np.float32)

    def place_entry(at, state, mode, low, high):
        rows[mode * 8 + low, 0, at] = 1.0
        cols[0, at, state * 8 + high] = 1.0
        if low != high:
            rows[mode * 8 + high, 1, at] = 1.0
            cols[1, at, state * 8 + low] = 1.0

    for at, state, mode, low, high in entries(row_units, 768):
        place_entry(at, state, mode, low, high)
    for lane, (at, state, mode, low, high) in enumerate(entries(col_units, 384)):
        pick[at, lane] = 1.0
        place_entry(1024 + lane, state, mode, low, high)
    rows = rows.reshape(64, 2560)
    cols = cols.reshape(2560, 128)
    return [jnp.asarray(value.astype(bf16)) for value in (pick, rows, cols)]


def shifted_sums(loads):
    sums = [None] * 5
    for value in loads:
        for shift in range(5):
            other = pltpu.roll(value, 8 - shift, 0) if shift else value
            part = value * other
            sums[shift] = part if sums[shift] is None else sums[shift] + part
    return sums


def three_mode_loads(ref, slot, width):
    step = width ** (2 - slot)
    lead = [0] if slot == 0 else [at * step * width for at in range(width**slot)]
    for first in lead:
        for inner in range(step):
            yield ref[pl.ds(first + inner, 8, stride=step), :]


def two_mode_loads(ref, lanes, start, slot, width):
    for inner in range(width):
        for low in lanes:
            if slot == 0:
                yield ref[low, pl.ds(start + inner, 8, stride=width), :]
            else:
                yield ref[low, pl.ds(start + inner * width, 8), :]


def lane_totals(parts, padded):
    if len(parts) * 8 < padded:
        parts = parts + [jnp.zeros((padded - 8 * len(parts), 128), f32)]
    stacked = split(jnp.concatenate(parts, axis=0))
    row = lax.broadcasted_iota(jnp.int32, (8, 128), 0)
    lane = lanes_of((8, 128))
    wanted = (row == 0) | ((row == 1) & (lane < 64)) | ((row == 2) & (lane >= 64))
    select = jnp.where(wanted, 1.0, 0.0).astype(bf16)
    totals = mm_nt(select, stacked[0]) + mm_nt(select, stacked[1])
    lane = lanes_of((1, padded))
    return jnp.where(lane < 120, totals[1:2], totals[0:1]), totals[2:3]


def pack_kernel(
    zero_ref, one_ref, two_ref, three_ref, send_ref, own_ref, items, tails, last, wide, middle, narrow
):
    items[...] = jnp.zeros((2, 256, 128), f32)
    tails[...] = jnp.zeros((1, 128, 128), f32)
    last[...] = jnp.zeros((1, 40, 128), f32)
    for lead in range(49):
        for row in range(2):
            start = 343 * lead
            at = 128 * row + lead
            half, place = divmod(lead, 25)
            place += 128 * row + 49
            for block in range(2):
                items[block, at : at + 1, :] = zero_ref[
                    row : row + 1, start + 128 * block : start + 128 * block + 128
                ]
            tail = zero_ref[row : row + 1, start + 256 : start + 343]
            items[half, place : place + 1, 0:87] = tail
            tails[0, 64 * row + lead : 64 * row + lead + 1, 0:87] = tail
    for lead in range(36):
        for ref, at in ((one_ref, 74 + lead), (two_ref, 202 + lead)):
            start = 216 * lead
            items[0, at : at + 1, :] = ref[0:1, start : start + 128]
            items[1, at : at + 1, 0:88] = ref[0:1, start + 128 : start + 216]
    for lead in range(25):
        half, place = divmod(lead, 13)
        value = three_ref[0:1, 125 * lead : 125 * lead + 125]
        items[half, 238 + place : 239 + place, 0:125] = value
        last[0, lead : lead + 1, 0:125] = value

    def turned(start):
        return jnp.concatenate([items[0, start : start + 128, :].T, items[1, start : start + 128, :].T])

    left, right = turned(0), turned(128)
    wide[0:384, :] = wide_from_items(left, 0, 0) + wide_from_items(right, 0, 64)
    wide[384:392, :] = jnp.zeros((8, 128), f32)
    middle[0:256, :] = moved_to(left, 74, 0, 36) + moved_to(right, 74, 64, 36)
    middle[256:288, :] = jnp.zeros((32, 128), f32)
    narrow[0:128, :] = narrow_from_items(right, 110, 0)
    narrow[128:200, :] = jnp.zeros((72, 128), f32)
    parts = []
    for ref, width in ((middle, 6), (wide, 7), (narrow, 5)):
        for slot in range(3):
            parts += shifted_sums(three_mode_loads(ref, slot, width))
    for slot in range(2):
        parts += shifted_sums(
            itertools.chain(
                two_mode_loads(items, (0, 1), 0, slot, 7),
                two_mode_loads(items, (0, 1), 128, slot, 7),
                two_mode_loads(tails, (0,), 0, slot, 7),
                two_mode_loads(tails, (0,), 64, slot, 7),
            )
        )
    for start in (74, 202):
        for slot in range(2):
            parts += shifted_sums(two_mode_loads(items, (0, 1), start, slot, 6))
    for slot in range(2):
        parts += shifted_sums(two_mode_loads(last, (0,), 0, slot, 5))
    first, second = lane_totals(parts, 768)
    for at in range(3):
        for block in range(2):
            low = 256 * at + 128 * block
            items[block, 110 + at : 111 + at, :] = first[:, low : low + 128]
    for block in range(2):
        items[block, 113:114, :] = second[:, 128 * block : 128 * block + 128]
    left = turned(0)
    own_ref[:, 0:128] = left
    own_ref[:, 128:256] = right
    send_ref[:, 0, 0:128] = left
    send_ref[:, 0, 128:256] = right


def lead_kernel(
    row_ref,
    col_ref,
    pair_ref,
    mode_ref,
    strength_ref,
    over_ref,
    pos_ref,
    intra_zero,
    intra_one,
    intra_two,
    intra_three,
    order_ref,
    *rest,
):
    out_refs, held, (mats, weights, sems) = rest[0:8], rest[8:16], rest[16:]
    la_high, la_low, lb_high, lb_low, lc_high, lc_low, ld_high, ld_low = held
    copies = [
        pltpu.make_async_copy(held[at], out_refs[at], sems.at[at]) for at in range(8)
    ]
    lists = Lists(row_ref, col_ref)
    fill_weights(pair_ref, mode_ref, strength_ref, weights)
    both = [(pair, flipped, range(3)) for pair in range(3) for flipped in (False, True)]
    fill_coupling(mats, over_ref, pos_ref, weights, both)
    fill_operators(mats, (intra_zero, intra_one, intra_two, intra_three), range(3))
    la = functools.partial(store_split, la_high, la_low)
    lb = functools.partial(store_split, lb_high, lb_low)
    lc = functools.partial(store_split, lc_high, lc_low)
    ld = functools.partial(store_split, ld_high, ld_low)
    even, odd, one, three = (list_at[name] for name in ("e", "o", "r1", "r3"))

    def kron(pair, rows, cols, flipped):
        return kron_three(lists, mats, pair, (0, 1, 2), rows, cols, flipped)

    def own(state, rows, cols):
        return sum_slots(lists, mats, 96 + 8 * state, 3, rows, cols)

    def tile(store, row, col, value):
        store((256 * row, 256), (256 * col, 256), value)

    for col, source in enumerate((even, odd)):
        zero_part, one_part = kron(0, one, source, True)
        tile(la, 0, col, zero_part)
        tile(la, 1, col, one_part)
    zero_part, one_part = kron(2, three, one, True)
    tile(la, 0, 2, zero_part)
    tile(la, 1, 2, one_part)
    zero_part, one_part = kron(2, one, three, False)
    tile(la, 0, 3, zero_part)
    tile(la, 1, 3, one_part)
    tile(la, 2, 0, own(0, odd, even))
    tile(la, 2, 1, own(0, odd, odd))
    tile(la, 2, 2, own(2, one, one))
    tile(la, 2, 3, own(3, three, three))
    copies[0].start()
    copies[1].start()
    tile(lb, 0, 0, own(0, even, even))
    tile(lb, 0, 1, own(0, even, odd))
    tile(lb, 0, 2, own(1, one, one))
    copies[2].start()
    copies[3].start()
    zero_part, one_part = kron(0, even, one, False)
    tile(lc, 0, 0, zero_part)
    tile(lc, 0, 1, one_part)
    zero_part, one_part = kron(0, odd, one, False)
    tile(lc, 0, 2, zero_part)
    tile(lc, 1, 2, one_part)
    zero_part, one_part = kron(1, one, one, True)
    tile(lc, 1, 0, zero_part)
    tile(lc, 1, 1, one_part)
    copies[4].start()
    copies[5].start()
    zero_part, one_part = kron(1, one, one, False)
    tile(ld, 0, 0, zero_part)
    tile(ld, 0, 1, one_part)
    copies[6].start()
    copies[7].start()
    for copy in copies:
        copy.wait()


def received_blocks(recv_ref):
    return recv_ref[:, 0, 0:128], recv_ref[:, 0, 128:256]


def middle_kernel(recv_ref, pick_ref, *rest):
    in_refs, send_ref, held = rest[0:8], rest[8], rest[9:17]
    wide, middle, narrow, sems = rest[17:]
    copies = [pltpu.make_async_copy(in_refs[at], held[at], sems.at[at]) for at in range(8)]
    for copy in copies:
        copy.start()
    left, right = received_blocks(recv_ref)
    wide[pl.ds(0, 172, stride=2), :] = keep(left[0:172], 0, 74)
    wide[pl.ds(1, 172, stride=2), :] = keep(right[0:172], 0, 74)
    wide[344:392, :] = jnp.zeros((48, 128), f32)
    middle[0:256, :] = moved_to(left, 74, 0, 36) + moved_to(right, 74, 64, 36)
    middle[256:288, :] = jnp.zeros((32, 128), f32)
    narrow[...] = keep(right[0:200], 110, 123)
    parts = []
    for ref, width in ((middle, 6), (wide, 7), (narrow, 5)):
        for slot in range(3):
            parts += shifted_sums(three_mode_loads(ref, slot, width))
    first, second = lane_totals(parts, 384)
    entries = split(jnp.concatenate([first, second[:, 0:128]], axis=1))
    picked = mm(entries[0], pick_ref[...]) + mm(entries[1], pick_ref[...])
    send_ref[:, 0, 896:1152] = jnp.broadcast_to(picked, (256, 256))
    summed = moved_to(jnp.sum(left, axis=0, keepdims=True), 110, 72, 4)

    even, odd = split(keep(left, 0, 74)), split(keep(right, 0, 74))
    one_at = [split(moved_to(left, 74, target, 36)) for target in (74, 0, 36, 72)]
    two_at = [split(moved_to(right, 74, target, 36)) for target in (74, 0, 36)]
    three = split(keep(right, 110, 123))

    def product(at, stack):
        copies[at].wait()
        copies[at + 1].wait()
        high = jnp.concatenate([part[0] for part in stack], axis=0)
        low = jnp.concatenate([part[1] for part in stack], axis=0)
        return mm3((held[at][...], held[at + 1][...]), (high, low))

    value = product(0, [even, odd, two_at[0], three])
    send_ref[:, 0, 0:128] = value[0:256]
    send_ref[:, 0, 128:256] = value[256:512]
    send_ref[:, 0, 384:512] = value[512:768]
    send_ref[:, 0, 256:384] = product(2, [even, odd, one_at[0]])
    value = product(4, one_at[1:])
    send_ref[:, 0, 512:640] = value[0:256]
    send_ref[:, 0, 640:768] = value[256:512]
    send_ref[:, 0, 768:896] = product(6, two_at[1:]) + summed


directions = (
    (0, False, "b0", "b1", "p6", "t7"),
    (0, True, "b1", "b0", "p7", "t6"),
    (1, False, "b1", "b1", "p6", "t6"),
    (1, True, "b1", "b1", "p6", "t6"),
    (2, False, "b1", "b3", "p5", "t6"),
    (2, True, "b3", "b1", "p6", "t5"),
)


homes = ((0, "b0", "t7"), (1, "b1", "t6"), (2, "b1", "t6"), (3, "b3", "t5"))


def tail_kernel(
    row_ref,
    col_ref,
    lane_ref,
    lcol_ref,
    pair_ref,
    mode_ref,
    strength_ref,
    over_ref,
    pos_ref,
    intra_zero,
    intra_one,
    intra_two,
    intra_three,
    own_ref,
    order_ref,
    *rest,
):
    outs, (mats, weights) = rest[:-2], rest[-2:]
    lists, lanes = Lists(row_ref, col_ref), Lists(lane_ref, lcol_ref)
    fill_weights(pair_ref, mode_ref, strength_ref, weights)
    wanted = []
    for pair, flipped, *_ in directions:
        wanted += [(pair, flipped, (5, 6, 7)), (pair, not flipped, (3, 4))]
    fill_coupling(mats, over_ref, pos_ref, weights, wanted)
    row = lax.broadcasted_iota(jnp.int32, (128, 128), 0)
    for at, (pair, flipped, target, source, from_lanes, to_lanes) in enumerate(directions):
        three_high, three_low, two_high, two_low = outs[4 * at : 4 * at + 4]
        rows, cols = list_at[target], list_at[source]
        over, moved = kron_three(lists, mats, pair, (5, 6, 7), rows, cols, flipped)
        store_split(three_high, three_low, (0, rows[1]), (0, cols[1]), over)
        store_split(three_high, three_low, (rows[1], rows[1]), (0, cols[1]), moved)
        lanes_in = (128 * lane_kinds[from_lanes], 128)
        lanes_out = (128 * lane_kinds[to_lanes], 128)
        base = pair * 32 + (0 if flipped else 16) + 3

        def factor(slot, extra):
            return expand(lanes, slot, lanes_in, mats[base + extra + slot], lanes_out)

        first, second = factor(0, 0), factor(1, 0)
        over = first * second
        moved = factor(0, 8) * second + first * factor(1, 8)
        store_split(two_high, two_low, (0, 128), (0, 128), jnp.where(row < 64, moved, over))
        store_split(two_high, two_low, (128, 128), (0, 128), jnp.where(row < 64, over, 0.0))
    home_ref = outs[-1]
    for state, ref in enumerate((intra_zero, intra_one, intra_two, intra_three)):
        for mode in range(3, 8):
            value = ref[:, mode, :]
            put_matrix(mats, 96 + 8 * state + mode, value.T if mode < 5 else value)
    views = own_views(own_ref)
    start = 0
    for state, index, kind in homes:
        at = list_at[index]
        span = (128 * lane_kinds[kind], 128)
        three = split(sum_slots(lists, mats, 96 + 8 * state + 5, 3, at, at))
        two = split(sum_slots(lanes, mats, 96 + 8 * state + 3, 2, span, span))
        if state == 0:
            mixed = mm3(three, split(jnp.concatenate(views[0:2], axis=1)))
            home_ref[0:384, :] = mixed[:, 0:128] + mm3(split(views[0]), two)
            home_ref[384:768, :] = mixed[:, 128:256] + mm3(split(views[1]), two)
            start = 768
        else:
            parts = split(views[state + 1])
            home_ref[pl.ds(start, at[1]), :] = mm3(three, parts) + mm3(parts, two)
            start += at[1]


def last_kernel(back_ref, own_ref, home_ref, rows_ref, cols_ref, *rest):
    tails, rest = rest[:24], rest[24:]
    zero_ref, one_ref, two_ref, three_ref, *density_refs = rest[:8]
    items = rest[8]
    seventh = back_ref[:, 0, 768:896]
    total = jnp.sum(back_ref[:, 0, 896:1152], axis=0, keepdims=True)
    density = jnp.zeros((64, 128), f32)
    for side in range(2):
        for at in range(4):
            span = slice(1280 * side + 256 * at, 1280 * side + 256 * at + 256)
            scaled = split(cols_ref[span, :].astype(f32) * seventh[:, 72 + at : 73 + at])
            density += mm(rows_ref[:, span], scaled[0]) + mm(rows_ref[:, span], scaled[1])
        span = slice(1280 * side + 1024, 1280 * side + 1280)
        scaled = split(rows_ref[:, span].astype(f32) * total)
        density += mm(scaled[0], cols_ref[span, :]) + mm(scaled[1], cols_ref[span, :])
    for state, ref in enumerate(density_refs):
        width = widths[state]
        value = density * (1.0 / float(width**7))
        for mode in range(8):
            ref[:, mode, :] = value[mode * 8 : mode * 8 + width, state * 8 : state * 8 + width]

    def block(at):
        return back_ref[:, 0, 128 * at : 128 * at + 128]

    first, second, fifth, sixth = block(0), block(1), block(4), block(5)
    even_in = moved_to(fifth, 0, 0, 36) + moved_to(fifth, 36, 64, 36)
    odd_in = moved_to(fifth, 72, 0, 36) + moved_to(sixth, 72, 64, 36)
    inputs = (
        jnp.concatenate([even_in, odd_in], axis=1),
        wide_from_items(first, 0, 0) + wide_from_items(second, 0, 64),
        moved_to(seventh, 0, 0, 36) + moved_to(seventh, 36, 64, 36),
        moved_to(sixth, 0, 0, 36) + moved_to(sixth, 36, 64, 36),
        narrow_from_items(first, 110, 0) + narrow_from_items(second, 110, 64),
        moved_to(first, 74, 0, 36) + moved_to(second, 74, 64, 36),
    )
    sums = {}
    targets = (("e", "o"), ("one",), ("one",), ("two",), ("two",), ("three",))
    for at, value in enumerate(inputs):
        three_high, three_low, two_high, two_low = tails[4 * at : 4 * at + 4]
        height = three_high.shape[0] // 2
        middle = mm3((three_high[...], three_low[...]), split(value))
        for which, name in enumerate(targets[at]):
            lanes = slice(128 * which, 128 * which + 128)
            both = jnp.concatenate([middle[0:height, lanes], middle[height:, lanes]], axis=1)
            part = mm3(split(both), (two_high[...], two_low[...]))
            sums[name] = part if name not in sums else sums[name] + part
    start = 0
    for name, height in (("e", 384), ("o", 384), ("one", 256), ("two", 256), ("three", 128)):
        sums[name] = sums[name] + home_ref[pl.ds(start, height), :]
        start += height
    left = items_from_wide(sums["e"]) + moved_to(sums["one"], 0, 74, 36) + block(2)
    right = (
        items_from_wide(sums["o"])
        + moved_to(sums["two"], 0, 74, 36)
        + items_from_narrow(sums["three"])
        + block(3)
    )
    items[0:128, :] = (own_ref[:, 0:128] - time_step * left).T
    items[128:256, :] = (own_ref[:, 128:256] - time_step * right).T
    for lead in range(49):
        for row in range(2):
            start = 343 * lead
            at = 128 * row
            zero_ref[row : row + 1, start : start + 256] = items[at + lead : at + lead + 1, 0:256]
            place, half = (lead, 0) if lead < 25 else (lead - 25, 128)
            zero_ref[row : row + 1, start + 256 : start + 343] = items[
                at + 49 + place : at + 50 + place, half : half + 87
            ]
    for lead in range(36):
        start = 216 * lead
        one_ref[0:1, start : start + 216] = items[74 + lead : 75 + lead, 0:216]
        two_ref[0:1, start : start + 216] = items[202 + lead : 203 + lead, 0:216]
    for lead in range(25):
        start = 125 * lead
        place, half = (lead, 0) if lead < 13 else (lead - 13, 128)
        three_ref[0:1, start : start + 125] = items[238 + place : 239 + place, half : half + 125]


def local(*args):
    states = args[:4]
    intra = [jnp.transpose(value, (1, 0, 2)) for value in args[4:8]]
    over, pos = (jnp.transpose(value, (0, 2, 1, 3)) for value in args[8:10])
    pair, mode, strength = args[10:]
    tables = [jnp.asarray(table) for table in digit_tables()]
    pick, density_rows, density_cols = density_tables()
    vm = pl.BlockSpec(memory_space=pltpu.VMEM)
    sm = pl.BlockSpec(memory_space=pltpu.SMEM)
    hbm = pl.BlockSpec(memory_space=pl.ANY)

    def call(kernel, operands, outs, scratch=(), specs=None, out_specs=None):
        return pl.pallas_call(
            kernel,
            out_shape=[jax.ShapeDtypeStruct(shape, kind) for shape, kind in outs],
            in_specs=specs or [vm] * len(operands),
            out_specs=out_specs or [vm] * len(outs),
            scratch_shapes=list(scratch),
            compiler_params=pltpu.CompilerParams(vmem_limit_bytes=vmem_limit),
        )(*operands)

    def exchange(value):
        return lax.all_to_all(value, axes, split_axis=0, concat_axis=0, tiled=True)

    column = [pltpu.VMEM((392, 128), f32), pltpu.VMEM((288, 128), f32), pltpu.VMEM((200, 128), f32)]
    with jax.named_scope("pack"):
        send, own = call(
            pack_kernel,
            states,
            [((256, 1, 256), f32), ((256, 256), f32)],
            [
                pltpu.VMEM((2, 256, 128), f32),
                pltpu.VMEM((1, 128, 128), f32),
                pltpu.VMEM((1, 40, 128), f32),
                *column,
            ],
        )
    with jax.named_scope("forward"):
        recv = exchange(send)
    mats = [pltpu.VMEM((mats_count, 24, 8), f32), pltpu.SMEM((24,), f32)]
    lead_shapes = []
    for shape in ((768, 1024), (256, 768), (512, 768), (256, 512)):
        lead_shapes += [shape] * 2
    held = [pltpu.VMEM(shape, bf16) for shape in lead_shapes]
    with jax.named_scope("lead_matrices"):
        lead = call(
            lead_kernel,
            [*tables[:2], pair, mode, strength, over, pos, *intra, own],
            [(shape, bf16) for shape in lead_shapes],
            [*held, *mats, pltpu.SemaphoreType.DMA((8,))],
            [vm] * 2 + [sm] * 3 + [vm] * 6 + [hbm],
            [hbm] * 8,
        )
    with jax.named_scope("lead_products"):
        (outgoing,) = call(
            middle_kernel,
            [recv, pick, *lead],
            [((256, 1, 1152), f32)],
            [*held, *column, pltpu.SemaphoreType.DMA((8,))],
            [vm] * 2 + [hbm] * 8,
        )
    with jax.named_scope("back"):
        back = exchange(outgoing)
    with jax.named_scope("tail_matrices"):
        tail_outs = []
        for pair_at, flipped, target, source, from_lanes, to_lanes in directions:
            tail_outs += [((2 * list_at[target][1], list_at[source][1]), bf16)] * 2
            tail_outs += [((256, 128), bf16)] * 2
        *tails, home = call(
            tail_kernel,
            [*tables, pair, mode, strength, over, pos, *intra, own, outgoing],
            tail_outs + [((1408, 128), f32)],
            mats,
            [vm] * 4 + [sm] * 3 + [vm] * 7 + [hbm],
        )
    with jax.named_scope("tail_products"):
        outs = call(
            last_kernel,
            [back, own, home, density_rows, density_cols, *tails],
            [(state.shape, f32) for state in states]
            + [((width, 8, width), f32) for width in widths],
            [pltpu.VMEM((256, 256), f32)],
        )
    densities = [jnp.transpose(value, (1, 0, 2)) for value in outs[4:]]
    return (*outs[:4], *densities)


def solution(mesh):
    rows = P(axes, None)
    in_specs = (rows,) * 4 + (P(),) * 9
    out_specs = (rows,) * 4 + (P(),) * 4
    return jax.shard_map(local, mesh=mesh, in_specs=in_specs, out_specs=out_specs, check_vma=False)
```

```python
import functools
import itertools

import jax
import jax.numpy as jnp
import numpy as np
from jax import lax
from jax.experimental import pallas as pl
from jax.experimental.pallas import tpu as pltpu
from jax.sharding import PartitionSpec as P

time_step = 0.25
axes = ("grp", "sub")
bf16 = jnp.bfloat16
f32 = jnp.float32
vmem_limit = 56 * 1024 * 1024
widths = (7, 6, 6, 5)

list_at = {"e": (0, 256), "o": (256, 256), "r1": (512, 256), "r3": (768, 256), "b0": (1024, 384)}
list_at["b1"] = list_at["r1"]
list_at["b3"] = (768, 128)
list_rows = 1408
target_rows = {"b0": 352, "b1": 224, "b3": 128}
lead_shapes = [shape for shape in ((672, 768), (224, 640), (400, 768), (224, 512)) for _ in range(2)]
spare_lanes = ((123, 128), (123, 128), (110, 128), (123, 128), (108, 128), (108, 128), (76, 128), (0, 128))
lane_kinds = {"p7": 0, "p6": 1, "p5": 2, "t7": 3, "t6": 4, "t5": 5}


def digit_tables():
    row_digits = np.full((list_rows, 3), -1)

    def fill(start, values, width):
        for place, value in enumerate(values):
            if 0 <= value < width**3:
                row_digits[start + place] = (value // width**2, value // width % width, value % width)

    fill(0, [2 * place for place in range(256)], 7)
    fill(256, [2 * place + 1 for place in range(256)], 7)
    fill(512, list(range(256)), 6)
    fill(768, list(range(256)), 5)
    fill(1024, list(range(384)), 7)
    lane_digits = np.full((768, 2), -1)
    for kind, at in lane_kinds.items():
        width = int(kind[1])
        for lane in range(128):
            value = lane % 64 if kind[0] == "p" else lane
            if value < width**2:
                lane_digits[128 * at + lane] = (value // width, value % width)

    def table(digits, invalid):
        total = np.full((digits.shape[0], 8), float(invalid), np.float32)
        valid = digits[:, 0] >= 0
        for slot in range(digits.shape[1]):
            value = np.zeros(digits.shape[0])
            for other in range(digits.shape[1]):
                if other != slot:
                    value = value * 8 + digits[:, other]
            total[:, slot] = np.where(valid, digits[:, slot], invalid)
            total[:, 3 + slot] = np.where(valid, value, invalid)
        return total

    return (
        table(row_digits, -1),
        np.ascontiguousarray(table(row_digits, -2).T),
        table(lane_digits, -1),
        np.ascontiguousarray(table(lane_digits, -2).T),
    )


class Lists:
    def __init__(self, row_ref, col_ref):
        self.row_ref, self.col_ref, self.made = row_ref, col_ref, {}

    def once(self, key, make):
        if key not in self.made:
            self.made[key] = make()
        return self.made[key]

    def rows_hot(self, slot, rows):
        def make():
            lane = lax.broadcasted_iota(jnp.int32, (rows[1], 24), 1) & 7
            digit = self.row_ref[pl.ds(*rows), slot : slot + 1]
            return jnp.where(digit == lane.astype(f32), 1.0, 0.0).astype(bf16)

        return self.once(("r", slot, rows), make)

    def cols_hot(self, slot, cols):
        def make():
            place = lax.broadcasted_iota(jnp.int32, (8, cols[1]), 0)
            digit = self.col_ref[slot : slot + 1, pl.ds(*cols)]
            return jnp.where(digit == place.astype(f32), 1.0, 0.0).astype(bf16)

        return self.once(("c", slot, cols), make)

    def same(self, slot, rows, cols):
        left = self.row_ref[pl.ds(*rows), 3 + slot : 4 + slot]
        return left == self.col_ref[3 + slot : 4 + slot, pl.ds(*cols)]


def mm(left, right):
    return jnp.dot(left, right, preferred_element_type=f32)


def mm_nt(left, right):
    return lax.dot_general(left, right, (((1,), (1,)), ((), ())), preferred_element_type=f32)


def split(value):
    high = value.astype(bf16)
    return high, (value - high.astype(f32)).astype(bf16)


def mm3(left, right):
    return mm(left[0], right[0]) + mm(left[0], right[1]) + mm(left[1], right[0])


def mm_wide(left, right):
    both = mm(left[0], jnp.concatenate(right, axis=1))
    return both[:, 0:128] + both[:, 128:256] + mm(left[1], right[0])


def taller(value, rows):
    return jnp.concatenate([value, jnp.zeros((rows - value.shape[0], 128), f32)], axis=0)


def put_matrix(mats, at, value):
    rows, columns = value.shape
    high = value.astype(bf16).astype(f32)
    middle = (value - high).astype(bf16).astype(f32)
    mats[at] = jnp.zeros((24, 8), f32)
    mats[at, 0:rows, 0:columns] = high
    mats[at, 8 : 8 + rows, 0:columns] = middle
    mats[at, 16 : 16 + rows, 0:columns] = value - high - middle


def expand(lists, slot, rows, matrix, cols):
    right = mm(matrix.astype(bf16), lists.cols_hot(slot, cols)).astype(bf16)
    return mm(lists.rows_hot(slot, rows), right)


def fill_weights(pair_ref, mode_ref, strength_ref, weights):
    for at in range(24):
        weights[at] = 0.0
    for term in range(24):
        at = pair_ref[term] * 8 + mode_ref[term]
        weights[at] = weights[at] + strength_ref[term]


mats_count = 128


def fill_coupling(mats, over_ref, pos_ref, weights, wanted):
    for pair, flipped, modes in wanted:
        for mode in modes:
            over = over_ref[pair, :, mode, :]
            moved = weights[pair * 8 + mode] * pos_ref[pair, :, mode, :]
            at = pair * 32 + mode
            if flipped:
                over, moved, at = over.T, moved.T, at + 16
            put_matrix(mats, at, over)
            put_matrix(mats, at + 8, moved)


def fill_operators(mats, refs, modes):
    for state, ref in enumerate(refs):
        for mode in modes:
            put_matrix(mats, 96 + 8 * state + mode, ref[:, mode, :])


def kron_three(lists, mats, pair, modes, rows, cols, flipped):
    base = pair * 32 + (16 if flipped else 0)

    def factor(slot, extra):
        return expand(lists, slot, rows, mats[base + extra + modes[slot]], cols)

    over_tail, over_mid = factor(2, 0), factor(1, 0)
    tail = over_mid * over_tail
    moved = factor(1, 8) * over_tail + over_mid * factor(2, 8)
    over_lead = factor(0, 0)
    return over_lead * tail, factor(0, 8) * tail + over_lead * moved


def sum_slots(lists, mats, at, slots, rows, cols, turned=False):
    total = None
    for slot in range(slots):
        matrix = mats[at + slot]
        part = expand(lists, slot, rows, matrix, cols)
        part = jnp.where(lists.same(slot, rows, cols), part, 0.0)
        total = part if total is None else total + part
    return total


def store_split(high_ref, low_ref, rows, cols, value):
    high, low = split(value)
    high_ref[pl.ds(*rows), pl.ds(*cols)] = high
    low_ref[pl.ds(*rows), pl.ds(*cols)] = low


def lanes_of(shape):
    return lax.broadcasted_iota(jnp.int32, shape, 1)


def keep(value, low, high):
    lane = lanes_of(value.shape)
    return jnp.where((lane >= low) & (lane < high), value, 0.0)


def moved_to(value, source, target, count):
    shift = (target - source) % 128
    if shift:
        value = pltpu.roll(value, shift, 1)
    return keep(value, target, target + count)


def wide_from_items(value, source, target):
    head = moved_to(value, source, target, 49)
    tail = moved_to(value[0:128], source + 49, target, 25) + moved_to(
        value[128:256], source + 49, target + 25, 24
    )
    return jnp.concatenate([head, tail], axis=0)


def items_from_wide(value):
    head = keep(value[0:256], 0, 49)
    tail = value[256:384]
    low = moved_to(tail, 0, 49, 25)
    high = moved_to(tail, 25, 49, 24)
    return head + jnp.concatenate([low, high], axis=0)


def narrow_from_items(value, source, target):
    return moved_to(value[0:128], source, target, 13) + moved_to(
        value[128:256], source, target + 13, 12
    )


def items_from_narrow(value):
    return jnp.concatenate([moved_to(value, 0, 110, 13), moved_to(value, 13, 110, 12)], axis=0)


def items_of(sums):
    left = items_from_wide(taller(sums["e"], 384)) + moved_to(taller(sums["one"], 256), 0, 74, 36)
    right = (
        items_from_wide(taller(sums["o"], 384))
        + moved_to(taller(sums["two"], 256), 0, 74, 36)
        + items_from_narrow(sums["three"])
    )
    return left, right


def own_views(own_ref):
    left, right = own_ref[:, 0:128], own_ref[:, 128:256]
    return (
        wide_from_items(left, 0, 0),
        wide_from_items(right, 0, 0),
        moved_to(left, 74, 0, 36),
        moved_to(right, 74, 0, 36),
        narrow_from_items(right, 110, 0),
    )


row_units = (
    [((1, 2), mode) for mode in (5, 6, 7)]
    + [((0,), mode) for mode in (5, 6, 7)]
    + [((3,), mode) for mode in (5, 6, 7)]
    + [((state,), mode) for state in range(4) for mode in (3, 4)]
)
col_units = [(states, mode) for states in ((1, 2), (0,), (3,)) for mode in (0, 1, 2)]


def density_tables():
    def entries(units, second):
        listed = []
        for unit, (states, mode) in enumerate(units):
            for half, state in enumerate(states):
                width = widths[state]
                for low in range(width):
                    for high in range(low, width):
                        shift = high - low
                        place = shift * 8 + low if shift <= 4 else (8 - shift) * 8 + high
                        listed.append((second * half + 40 * unit + place, state, mode, low, high))
        return listed

    pick = np.zeros((512, 1024), np.float32)
    rows = np.zeros((64, 2, 2048), np.float32)
    cols = np.zeros((2, 2048, 128), np.float32)

    def place_entry(at, state, mode, low, high):
        rows[mode * 8 + low, 0, at] = 1.0
        cols[0, at, state * 8 + high] = 1.0
        if low != high:
            rows[mode * 8 + high, 1, at] = 1.0
            cols[1, at, state * 8 + low] = 1.0
        elif state == 0 and mode in (0, 1, 3):
            cols[1, at, 6] = 1.0
            if mode == 3:
                rows[6, 1, at] = rows[14, 1, at] = 1.0
            else:
                rows[mode * 8 + 6, 1, at] = -1.0

    for entry in entries(row_units, 768):
        place_entry(*entry)
    lanes = iter(
        128 * block + lane for block, span in enumerate(spare_lanes) for lane in range(*span)
    )
    for at, state, mode, low, high in entries(col_units, 384):
        if state == 0 and mode < 2 and low == 6:
            continue
        lane = next(lanes)
        pick[at, lane] = 1.0
        place_entry(1024 + lane, state, mode, low, high)
    rows = rows.reshape(64, 4096)
    cols = cols.reshape(4, 1024, 128)[:, :, 0:32].transpose(1, 0, 2).reshape(1024, 128)
    return [jnp.asarray(value.astype(bf16)) for value in (pick, rows, cols)]


def shifted_sums(loads):
    sums = [None] * 5
    for value in loads:
        for shift in range(5):
            other = pltpu.roll(value, 8 - shift, 0) if shift else value
            part = value * other
            sums[shift] = part if sums[shift] is None else sums[shift] + part
    return sums


def three_mode_loads(ref, slot, width):
    step = width ** (2 - slot)
    lead = [0] if slot == 0 else [at * step * width for at in range(width**slot)]
    for first in lead:
        for inner in range(step):
            yield ref[pl.ds(first + inner, 8, stride=step), :]


def two_mode_loads(ref, lanes, start, slot, width):
    for inner in range(width):
        for low in lanes:
            if slot == 0:
                yield ref[low, pl.ds(start + inner, 8, stride=width), :]
            else:
                yield ref[low, pl.ds(start + inner * width, 8), :]


def lane_totals(parts, padded):
    if len(parts) * 8 < padded:
        parts = parts + [jnp.zeros((padded - 8 * len(parts), 128), f32)]
    stacked = split(jnp.concatenate(parts, axis=0))
    row = lax.broadcasted_iota(jnp.int32, (8, 128), 0)
    lane = lanes_of((8, 128))
    wanted = (row == 0) | ((row == 1) & (lane < 64)) | ((row == 2) & (lane >= 64))
    select = jnp.where(wanted, 1.0, 0.0).astype(bf16)
    totals = mm_nt(select, stacked[0]) + mm_nt(select, stacked[1])
    lane = lanes_of((1, padded))
    return jnp.where(lane < 120, totals[1:2], totals[0:1]), totals[2:3]


def pack_kernel(
    zero_ref, one_ref, two_ref, three_ref, send_ref, own_ref, items, tails, last, wide, middle, narrow
):
    items[...] = jnp.zeros((2, 256, 128), f32)
    tails[...] = jnp.zeros((1, 128, 128), f32)
    last[...] = jnp.zeros((1, 40, 128), f32)
    for lead in range(49):
        for row in range(2):
            start = 343 * lead
            at = 128 * row + lead
            half, place = divmod(lead, 25)
            place += 128 * row + 49
            for block in range(2):
                items[block, at : at + 1, :] = zero_ref[
                    row : row + 1, start + 128 * block : start + 128 * block + 128
                ]
            tail = zero_ref[row : row + 1, start + 256 : start + 343]
            items[half, place : place + 1, 0:87] = tail
            tails[0, 64 * row + lead : 64 * row + lead + 1, 0:87] = tail
    for lead in range(36):
        for ref, at in ((one_ref, 74 + lead), (two_ref, 202 + lead)):
            start = 216 * lead
            items[0, at : at + 1, :] = ref[0:1, start : start + 128]
            items[1, at : at + 1, 0:88] = ref[0:1, start + 128 : start + 216]
    for lead in range(25):
        half, place = divmod(lead, 13)
        value = three_ref[0:1, 125 * lead : 125 * lead + 125]
        items[half, 238 + place : 239 + place, 0:125] = value
        last[0, lead : lead + 1, 0:125] = value

    def turned(start):
        return jnp.concatenate([items[0, start : start + 128, :].T, items[1, start : start + 128, :].T])

    left, right = turned(0), turned(128)
    wide[0:384, :] = wide_from_items(left, 0, 0) + wide_from_items(right, 0, 64)
    wide[384:392, :] = jnp.zeros((8, 128), f32)
    middle[0:256, :] = moved_to(left, 74, 0, 36) + moved_to(right, 74, 64, 36)
    middle[256:288, :] = jnp.zeros((32, 128), f32)
    narrow[0:128, :] = narrow_from_items(right, 110, 0)
    narrow[128:200, :] = jnp.zeros((72, 128), f32)
    parts = []
    for ref, width in ((middle, 6), (wide, 7), (narrow, 5)):
        for slot in range(3):
            parts += shifted_sums(three_mode_loads(ref, slot, width))
    for slot in range(2):
        parts += shifted_sums(
            itertools.chain(
                two_mode_loads(items, (0, 1), 0, slot, 7),
                two_mode_loads(items, (0, 1), 128, slot, 7),
                two_mode_loads(tails, (0,), 0, slot, 7),
                two_mode_loads(tails, (0,), 64, slot, 7),
            )
        )
    for start in (74, 202):
        for slot in range(2):
            parts += shifted_sums(two_mode_loads(items, (0, 1), start, slot, 6))
    for slot in range(2):
        parts += shifted_sums(two_mode_loads(last, (0,), 0, slot, 5))
    first, second = lane_totals(parts, 768)
    for at in range(3):
        for block in range(2):
            low = 256 * at + 128 * block
            items[block, 110 + at : 111 + at, :] = first[:, low : low + 128]
    for block in range(2):
        items[block, 113:114, :] = second[:, 128 * block : 128 * block + 128]
    left = turned(0)
    own_ref[:, 0:128] = left
    own_ref[:, 128:256] = right
    send_ref[:, 0, 0:128] = left
    send_ref[:, 0, 128:256] = right


def lead_kernel(
    row_ref,
    col_ref,
    pair_ref,
    mode_ref,
    strength_ref,
    over_ref,
    pos_ref,
    intra_zero,
    intra_one,
    intra_two,
    intra_three,
    order_ref,
    *rest,
):
    out_refs, held, (mats, weights, sems) = rest[0:8], rest[8:16], rest[16:]
    la_high, la_low, lb_high, lb_low, lc_high, lc_low, ld_high, ld_low = held
    copies = [
        pltpu.make_async_copy(held[at], out_refs[at], sems.at[at]) for at in range(8)
    ]
    lists = Lists(row_ref, col_ref)
    fill_weights(pair_ref, mode_ref, strength_ref, weights)
    both = [(pair, flipped, range(3)) for pair in range(3) for flipped in (False, True)]
    fill_coupling(mats, over_ref, pos_ref, weights, both)
    fill_operators(mats, (intra_zero, intra_one, intra_two, intra_three), range(3))
    la = functools.partial(store_split, la_high, la_low)
    lb = functools.partial(store_split, lb_high, lb_low)
    lc = functools.partial(store_split, lc_high, lc_low)
    ld = functools.partial(store_split, ld_high, ld_low)
    even, odd, one, three = ((list_at[name][0], 224) for name in ("e", "o", "r1", "r3"))
    from_zero, from_one, from_three = (list_at[name] for name in ("b0", "r1", "b3"))

    def kron(pair, rows, cols, flipped):
        return kron_three(lists, mats, pair, (0, 1, 2), rows, cols, flipped)

    def own(state, rows, cols):
        return sum_slots(lists, mats, 96 + 8 * state, 3, rows, cols)

    def tile(store, row, col, value):
        store((row, value.shape[0]), (col, value.shape[1]), value)

    zero_part, one_part = kron(0, one, from_zero, True)
    tile(la, 0, 0, zero_part)
    tile(la, 224, 0, one_part)
    zero_part, one_part = kron(2, three, from_one, True)
    tile(la, 0, 384, zero_part)
    tile(la, 224, 384, one_part)
    zero_part, one_part = kron(2, one, from_three, False)
    tile(la, 0, 640, zero_part)
    tile(la, 224, 640, one_part)
    tile(la, 448, 0, own(0, odd, from_zero))
    tile(la, 448, 384, own(2, one, from_one))
    tile(la, 448, 640, own(3, three, from_three))
    copies[0].start()
    copies[1].start()
    tile(lb, 0, 0, own(0, even, from_zero))
    tile(lb, 0, 384, own(1, one, from_one))
    copies[2].start()
    copies[3].start()
    zero_part, one_part = kron(0, (even[0], 176), from_one, False)
    tile(lc, 0, 0, zero_part)
    tile(lc, 0, 256, one_part)
    zero_part, one_part = kron(0, odd, from_one, False)
    tile(lc, 0, 512, zero_part[0:176])
    tile(lc, 176, 512, one_part)
    zero_part, one_part = kron(1, one, from_one, True)
    tile(lc, 176, 0, zero_part)
    tile(lc, 176, 256, one_part)
    copies[4].start()
    copies[5].start()
    zero_part, one_part = kron(1, one, from_one, False)
    tile(ld, 0, 0, zero_part)
    tile(ld, 0, 256, one_part)
    copies[6].start()
    copies[7].start()
    for copy in copies:
        copy.wait()


def received_blocks(recv_ref):
    return recv_ref[:, 0, 0:128], recv_ref[:, 0, 128:256]


def middle_kernel(recv_ref, pick_ref, *rest):
    in_refs, send_ref, held = rest[0:8], rest[8], rest[9:17]
    wide, middle, narrow, sems = rest[17:]
    copies = [pltpu.make_async_copy(in_refs[at], held[at], sems.at[at]) for at in range(8)]
    for copy in copies:
        copy.start()
    left, right = received_blocks(recv_ref)
    wide[pl.ds(0, 172, stride=2), :] = keep(left[0:172], 0, 74)
    wide[pl.ds(1, 172, stride=2), :] = keep(right[0:172], 0, 74)
    wide[344:392, :] = jnp.zeros((48, 128), f32)
    middle[0:256, :] = moved_to(left, 74, 0, 36) + moved_to(right, 74, 64, 36)
    middle[256:288, :] = jnp.zeros((32, 128), f32)
    narrow[...] = keep(right[0:200], 110, 123)
    parts = []
    for ref, width in ((middle, 6), (wide, 7), (narrow, 5)):
        for slot in range(3):
            parts += shifted_sums(three_mode_loads(ref, slot, width))
    first, second = lane_totals(parts, 384)
    entries = split(jnp.concatenate([first, second[:, 0:128]], axis=1))
    picked = mm(entries[0], pick_ref[...]) + mm(entries[1], pick_ref[...])
    summed = moved_to(jnp.sum(left, axis=0, keepdims=True), 110, 72, 4)

    def put(block, value):
        span = slice(128 * block, 128 * block + 128)
        extra = picked[:, span]
        if block == 6:
            extra = extra + summed
        rows = value.shape[0]
        send_ref[0:rows, 0, span] = value + extra
        send_ref[rows:256, 0, span] = jnp.broadcast_to(extra, (256 - rows, 128))

    from_zero = split(wide[0:384, :])
    one_at = [split(moved_to(left, 74, target, 36)) for target in (74, 0, 36, 72)]
    two_at = [split(moved_to(right, 74, target, 36)) for target in (74, 0, 36)]
    from_three = split(keep(right[0:128], 110, 123))

    def product(at, stack):
        copies[at].wait()
        copies[at + 1].wait()
        high = jnp.concatenate([part[0] for part in stack], axis=0)
        low = jnp.concatenate([part[1] for part in stack], axis=0)
        return mm_wide((held[at][...], held[at + 1][...]), (high, low))

    value = product(0, [from_zero, two_at[0], from_three])
    put(0, value[0:224])
    put(1, value[224:448])
    put(3, value[448:672])
    put(2, product(2, [from_zero, one_at[0]]))
    value = product(4, one_at[1:])
    put(4, value[0:176])
    put(5, value[176:400])
    put(6, product(6, two_at[1:]))
    send_ref[:, 0, 896:1024] = jnp.broadcast_to(picked[:, 896:1024], (256, 128))


directions = (
    (0, False, "b0", "b1", "p6", "t7"),
    (0, True, "b1", "b0", "p7", "t6"),
    (1, False, "b1", "b1", "p6", "t6"),
    (1, True, "b1", "b1", "p6", "t6"),
    (2, False, "b1", "b3", "p5", "t6"),
    (2, True, "b3", "b1", "p6", "t5"),
)


homes = ((0, "b0", "t7"), (1, "b1", "t6"), (2, "b1", "t6"), (3, "b3", "t5"))


def tail_kernel(
    row_ref,
    col_ref,
    lane_ref,
    lcol_ref,
    pair_ref,
    mode_ref,
    strength_ref,
    over_ref,
    pos_ref,
    intra_zero,
    intra_one,
    intra_two,
    intra_three,
    own_ref,
    order_ref,
    *rest,
):
    outs, (mats, weights) = rest[:-2], rest[-2:]
    lists, lanes = Lists(row_ref, col_ref), Lists(lane_ref, lcol_ref)
    fill_weights(pair_ref, mode_ref, strength_ref, weights)
    wanted = []
    for pair, flipped, *_ in directions:
        wanted += [(pair, flipped, (5, 6, 7)), (pair, not flipped, (3, 4))]
    fill_coupling(mats, over_ref, pos_ref, weights, wanted)
    row = lax.broadcasted_iota(jnp.int32, (128, 128), 0)
    for at, (pair, flipped, target, source, from_lanes, to_lanes) in enumerate(directions):
        three_high, three_low, two_ref = outs[3 * at : 3 * at + 3]
        rows, cols = (list_at[target][0], target_rows[target]), list_at[source]
        over, moved = kron_three(lists, mats, pair, (5, 6, 7), rows, cols, flipped)
        store_split(three_high, three_low, (0, rows[1]), (0, cols[1]), over)
        store_split(three_high, three_low, (rows[1], rows[1]), (0, cols[1]), moved)
        lanes_in = (128 * lane_kinds[from_lanes], 128)
        lanes_out = (128 * lane_kinds[to_lanes], 128)
        base = pair * 32 + (0 if flipped else 16) + 3

        def factor(slot, extra):
            return expand(lanes, slot, lanes_in, mats[base + extra + slot], lanes_out)

        first, second = factor(0, 0), factor(1, 0)
        over = first * second
        moved = factor(0, 8) * second + first * factor(1, 8)
        upper, lower = split(jnp.where(row < 64, moved, over)), split(jnp.where(row < 64, over, 0.0))
        for part in range(2):
            two_ref[0:128, 128 * part : 128 * part + 128] = upper[part]
            two_ref[128:256, 128 * part : 128 * part + 128] = lower[part]
    base_ref = outs[-1]
    sums = {}
    for state, ref in enumerate((intra_zero, intra_one, intra_two, intra_three)):
        for mode in range(3, 8):
            value = ref[:, mode, :]
            put_matrix(mats, 96 + 8 * state + mode, value.T if mode < 5 else value)
    views = own_views(own_ref)
    for state, index, kind in homes:
        rows, cols = (list_at[index][0], target_rows[index]), list_at[index]
        span = (128 * lane_kinds[kind], 128)
        three = split(sum_slots(lists, mats, 96 + 8 * state + 5, 3, rows, cols))
        two = split(sum_slots(lanes, mats, 96 + 8 * state + 3, 2, span, span))
        used = views[0:2] if state == 0 else views[state + 1 : state + 2]
        names = ("e", "o") if state == 0 else (("one", "two", "three")[state - 1],)
        for view, name in zip(used, names):
            sums[name] = mm_wide(three, split(view)) + mm_wide(split(view[0 : rows[1]]), two)
    left, right = items_of(sums)
    base_ref[:, 0:128] = own_ref[:, 0:128] - time_step * left
    base_ref[:, 128:256] = own_ref[:, 128:256] - time_step * right


def last_kernel(back_ref, *rest):
    count = 21
    in_refs, rest = rest[:count], rest[count:]
    zero_ref, one_ref, two_ref, three_ref, *density_refs = rest[:8]
    items, *held, sems = rest[8:]
    copies = [pltpu.make_async_copy(in_refs[at], held[at], sems.at[at]) for at in range(count)]
    for at in (19, 20, *range(19)):
        copies[at].start()
    base_ref, rows_ref, cols_ref = held[18:21]

    def block(at):
        return back_ref[:, 0, 128 * at : 128 * at + 128]

    first, second, fifth, sixth, seventh = (block(at) for at in (0, 1, 4, 5, 6))
    copies[19].wait()
    copies[20].wait()
    totals = []
    for at, span in enumerate(spare_lanes):
        totals.append(keep(jnp.sum(block(at), axis=0, keepdims=True), *span))
    total = jnp.concatenate(totals, axis=1)
    turned = seventh.T
    entries = jnp.concatenate([turned[72 + at : 73 + at, :] for at in range(4)] + [total], axis=1)
    quarters = []
    for quarter in range(4):
        part = entries[:, 1024 * (quarter % 2) : 1024 * (quarter % 2) + 1024]
        quarters.append(rows_ref[:, 1024 * quarter : 1024 * quarter + 1024].astype(f32) * part)
    high, low = split(jnp.concatenate(quarters, axis=0))
    placed = mm(high, cols_ref[...]) + mm(low, cols_ref[...])
    density = placed[0:64]
    for quarter in range(1, 4):
        density += pltpu.roll(placed[64 * quarter : 64 * quarter + 64], 128 - 32 * quarter, 1)
    for state, ref in enumerate(density_refs):
        width = widths[state]
        value = density * (1.0 / float(width**7))
        for mode in range(8):
            ref[:, mode, :] = value[mode * 8 : mode * 8 + width, state * 8 : state * 8 + width]

    even_in = moved_to(fifth, 0, 0, 36) + moved_to(fifth, 36, 64, 36)
    odd_in = moved_to(fifth, 72, 0, 36) + moved_to(sixth, 72, 64, 36)
    inputs = (
        jnp.concatenate([even_in, odd_in], axis=1),
        wide_from_items(first, 0, 0) + wide_from_items(second, 0, 64),
        moved_to(seventh, 0, 0, 36) + moved_to(seventh, 36, 64, 36),
        moved_to(sixth, 0, 0, 36) + moved_to(sixth, 36, 64, 36),
        narrow_from_items(first, 110, 0) + narrow_from_items(second, 110, 64),
        moved_to(first, 74, 0, 36) + moved_to(second, 74, 64, 36),
    )
    for copy in copies[0:19]:
        copy.wait()
    sums = {}
    targets = (("e", "o"), ("one",), ("one",), ("two",), ("two",), ("three",))
    for at, value in enumerate(inputs):
        three_high, three_low, two = held[3 * at : 3 * at + 3]
        height = three_high.shape[0] // 2
        product = mm_wide if value.shape[1] == 128 else mm3
        middle = product((three_high[...], three_low[...]), split(value))
        for which, name in enumerate(targets[at]):
            lanes = slice(128 * which, 128 * which + 128)
            both = split(jnp.concatenate([middle[0:height, lanes], middle[height:, lanes]], axis=1))
            part = mm(both[0], two[...])
            part = part[:, 0:128] + part[:, 128:256] + mm(both[1], two[:, 0:128])
            sums[name] = part if name not in sums else sums[name] + part
    left, right = items_of(sums)
    items[0:128, :] = (base_ref[:, 0:128] - time_step * (left + block(2))).T
    items[128:256, :] = (base_ref[:, 128:256] - time_step * (right + block(3))).T
    for lead in range(49):
        for row in range(2):
            start = 343 * lead
            at = 128 * row
            zero_ref[row : row + 1, start : start + 256] = items[at + lead : at + lead + 1, 0:256]
            place, half = (lead, 0) if lead < 25 else (lead - 25, 128)
            zero_ref[row : row + 1, start + 256 : start + 343] = items[
                at + 49 + place : at + 50 + place, half : half + 87
            ]
    for lead in range(36):
        start = 216 * lead
        one_ref[0:1, start : start + 216] = items[74 + lead : 75 + lead, 0:216]
        two_ref[0:1, start : start + 216] = items[202 + lead : 203 + lead, 0:216]
    for lead in range(25):
        start = 125 * lead
        place, half = (lead, 0) if lead < 13 else (lead - 13, 128)
        three_ref[0:1, start : start + 125] = items[238 + place : 239 + place, half : half + 125]


def local(*args):
    states = args[:4]
    intra = [jnp.transpose(value, (1, 0, 2)) for value in args[4:8]]
    over, pos = (jnp.transpose(value, (0, 2, 1, 3)) for value in args[8:10])
    pair, mode, strength = args[10:]
    tables = [jnp.asarray(table) for table in digit_tables()]
    pick, density_rows, density_cols = density_tables()
    vm = pl.BlockSpec(memory_space=pltpu.VMEM)
    sm = pl.BlockSpec(memory_space=pltpu.SMEM)
    hbm = pl.BlockSpec(memory_space=pl.ANY)

    def call(kernel, operands, outs, scratch=(), specs=None, out_specs=None):
        return pl.pallas_call(
            kernel,
            out_shape=[jax.ShapeDtypeStruct(shape, kind) for shape, kind in outs],
            in_specs=specs or [vm] * len(operands),
            out_specs=out_specs or [vm] * len(outs),
            scratch_shapes=list(scratch),
            compiler_params=pltpu.CompilerParams(vmem_limit_bytes=vmem_limit),
        )(*operands)

    def exchange(value):
        return lax.all_to_all(value, axes, split_axis=0, concat_axis=0, tiled=True)

    column = [pltpu.VMEM((392, 128), f32), pltpu.VMEM((288, 128), f32), pltpu.VMEM((200, 128), f32)]
    with jax.named_scope("pack"):
        send, own = call(
            pack_kernel,
            states,
            [((256, 1, 256), f32), ((256, 256), f32)],
            [
                pltpu.VMEM((2, 256, 128), f32),
                pltpu.VMEM((1, 128, 128), f32),
                pltpu.VMEM((1, 40, 128), f32),
                *column,
            ],
        )
    with jax.named_scope("forward"):
        recv = exchange(send)
    mats = [pltpu.VMEM((mats_count, 24, 8), f32), pltpu.SMEM((24,), f32)]
    held = [pltpu.VMEM(shape, bf16) for shape in lead_shapes]
    with jax.named_scope("lead_matrices"):
        lead = call(
            lead_kernel,
            [*tables[:2], pair, mode, strength, over, pos, *intra, own],
            [(shape, bf16) for shape in lead_shapes],
            [*held, *mats, pltpu.SemaphoreType.DMA((8,))],
            [vm] * 2 + [sm] * 3 + [vm] * 6 + [hbm],
            [hbm] * 8,
        )
    with jax.named_scope("lead_products"):
        (outgoing,) = call(
            middle_kernel,
            [recv, pick, *lead],
            [((256, 1, 1024), f32)],
            [*held, *column, pltpu.SemaphoreType.DMA((8,))],
            [vm] * 2 + [hbm] * 8,
        )
    with jax.named_scope("back"):
        back = exchange(outgoing)
    with jax.named_scope("tail_matrices"):
        tail_outs = []
        for pair_at, flipped, target, source, from_lanes, to_lanes in directions:
            tail_outs += [((2 * target_rows[target], list_at[source][1]), bf16)] * 2
            tail_outs.append(((256, 256), bf16))
        tail_outs.append(((256, 256), f32))
        tails = call(
            tail_kernel,
            [*tables, pair, mode, strength, over, pos, *intra, own, outgoing],
            tail_outs,
            mats,
            [vm] * 4 + [sm] * 3 + [vm] * 7 + [hbm],
        )
    with jax.named_scope("tail_products"):
        late = [*tails, density_rows, density_cols]
        outs = call(
            last_kernel,
            [back, *late],
            [(state.shape, f32) for state in states]
            + [((width, 8, width), f32) for width in widths],
            [
                pltpu.VMEM((256, 256), f32),
                *[pltpu.VMEM(value.shape, value.dtype) for value in late],
                pltpu.SemaphoreType.DMA((len(late),)),
            ],
            [vm] + [hbm] * len(late),
        )
    densities = [jnp.transpose(value, (1, 0, 2)) for value in outs[4:]]
    return (*outs[:4], *densities)


def solution(mesh):
    rows = P(axes, None)
    in_specs = (rows,) * 4 + (P(),) * 9
    out_specs = (rows,) * 4 + (P(),) * 4
    return jax.shard_map(local, mesh=mesh, in_specs=in_specs, out_specs=out_specs, check_vma=False)
```

```python
import functools
import itertools

import jax
import jax.numpy as jnp
import numpy as np
from jax import lax
from jax.experimental import pallas as pl
from jax.experimental.pallas import tpu as pltpu
from jax.sharding import PartitionSpec as P

time_step = 0.25
axes = ("grp", "sub")
bf16 = jnp.bfloat16
f32 = jnp.float32
widths = (7, 6, 6, 5)

list_at = {"e": (0, 256), "o": (256, 256), "r1": (512, 256), "r3": (768, 256), "b0": (1024, 384)}
list_at["b1"] = list_at["r1"]
list_at["b3"] = (768, 128)
list_rows = 1408
target_rows = {"b0": 352, "b1": 224, "b3": 128}
lead_shapes = [shape for shape in ((672, 768), (224, 1152), (400, 768)) for _ in range(2)]
spare_lanes = ((123, 128), (123, 128), (110, 128), (123, 128), (108, 128), (108, 128), (76, 128), (0, 128))
lane_kinds = {"p7": 0, "p6": 1, "p5": 2, "t7": 3, "t6": 4, "t5": 5}


def digit_tables():
    row_digits = np.full((list_rows, 3), -1)

    def fill(start, values, width):
        for place, value in enumerate(values):
            if 0 <= value < width**3:
                row_digits[start + place] = (value // width**2, value // width % width, value % width)

    fill(0, [2 * place for place in range(256)], 7)
    fill(256, [2 * place + 1 for place in range(256)], 7)
    fill(512, list(range(256)), 6)
    fill(768, list(range(256)), 5)
    fill(1024, list(range(384)), 7)
    lane_digits = np.full((768, 2), -1)
    for kind, at in lane_kinds.items():
        width = int(kind[1])
        for lane in range(128):
            value = lane % 64 if kind[0] == "p" else lane
            if value < width**2:
                lane_digits[128 * at + lane] = (value // width, value % width)

    def table(digits, invalid):
        total = np.full((digits.shape[0], 8), float(invalid), np.float32)
        valid = digits[:, 0] >= 0
        for slot in range(digits.shape[1]):
            value = np.zeros(digits.shape[0])
            for other in range(digits.shape[1]):
                if other != slot:
                    value = value * 8 + digits[:, other]
            total[:, slot] = np.where(valid, digits[:, slot], invalid)
            total[:, 3 + slot] = np.where(valid, value, invalid)
        return total

    return (
        table(row_digits, -1),
        np.ascontiguousarray(table(row_digits, -2).T),
        table(lane_digits, -1),
        np.ascontiguousarray(table(lane_digits, -2).T),
    )


class Lists:
    def __init__(self, row_ref, col_ref):
        self.row_ref, self.col_ref, self.made = row_ref, col_ref, {}

    def once(self, key, make):
        if key not in self.made:
            self.made[key] = make()
        return self.made[key]

    def rows_hot(self, slot, rows):
        def make():
            lane = lax.broadcasted_iota(jnp.int32, (rows[1], 24), 1) & 7
            digit = self.row_ref[pl.ds(*rows), slot : slot + 1]
            return jnp.where(digit == lane.astype(f32), 1.0, 0.0).astype(bf16)

        return self.once(("r", slot, rows), make)

    def cols_hot(self, slot, cols):
        def make():
            place = lax.broadcasted_iota(jnp.int32, (8, cols[1]), 0)
            digit = self.col_ref[slot : slot + 1, pl.ds(*cols)]
            return jnp.where(digit == place.astype(f32), 1.0, 0.0).astype(bf16)

        return self.once(("c", slot, cols), make)

    def same(self, slot, rows, cols):
        left = self.row_ref[pl.ds(*rows), 3 + slot : 4 + slot]
        return left == self.col_ref[3 + slot : 4 + slot, pl.ds(*cols)]


def mm(left, right):
    return jnp.dot(left, right, preferred_element_type=f32)


def mm_nt(left, right):
    return lax.dot_general(left, right, (((1,), (1,)), ((), ())), preferred_element_type=f32)


def split(value):
    high = value.astype(bf16)
    return high, (value - high.astype(f32)).astype(bf16)


def mm3(left, right):
    return mm(left[0], right[0]) + mm(left[0], right[1]) + mm(left[1], right[0])


def mm_wide(left, right):
    both = mm(left[0], jnp.concatenate(right, axis=1))
    return both[:, 0:128] + both[:, 128:256] + mm(left[1], right[0])


def taller(value, rows):
    return jnp.concatenate([value, jnp.zeros((rows - value.shape[0], 128), f32)], axis=0)


def put_matrix(mats, at, value):
    rows, columns = value.shape
    high = value.astype(bf16).astype(f32)
    middle = (value - high).astype(bf16).astype(f32)
    mats[at] = jnp.zeros((24, 8), f32)
    mats[at, 0:rows, 0:columns] = high
    mats[at, 8 : 8 + rows, 0:columns] = middle
    mats[at, 16 : 16 + rows, 0:columns] = value - high - middle


def expand(lists, slot, rows, matrix, cols):
    right = mm(matrix.astype(bf16), lists.cols_hot(slot, cols)).astype(bf16)
    return mm(lists.rows_hot(slot, rows), right)


def fill_weights(pair_ref, mode_ref, strength_ref, weights):
    for at in range(24):
        weights[at] = 0.0
    for term in range(24):
        at = pair_ref[term] * 8 + mode_ref[term]
        weights[at] = weights[at] + strength_ref[term]


mats_count = 128


def fill_coupling(mats, over_ref, pos_ref, weights, wanted):
    for pair, flipped, modes in wanted:
        for mode in modes:
            over = over_ref[pair, :, mode, :]
            moved = weights[pair * 8 + mode] * pos_ref[pair, :, mode, :]
            at = pair * 32 + mode
            if flipped:
                over, moved, at = over.T, moved.T, at + 16
            put_matrix(mats, at, over)
            put_matrix(mats, at + 8, moved)


def fill_operators(mats, refs, modes):
    for state, ref in enumerate(refs):
        for mode in modes:
            put_matrix(mats, 96 + 8 * state + mode, ref[:, mode, :])


def kron_three(lists, mats, pair, modes, rows, cols, flipped):
    base = pair * 32 + (16 if flipped else 0)

    def factor(slot, extra):
        return expand(lists, slot, rows, mats[base + extra + modes[slot]], cols)

    over_tail, over_mid = factor(2, 0), factor(1, 0)
    tail = over_mid * over_tail
    moved = factor(1, 8) * over_tail + over_mid * factor(2, 8)
    over_lead = factor(0, 0)
    return over_lead * tail, factor(0, 8) * tail + over_lead * moved


def sum_slots(lists, mats, at, slots, rows, cols, turned=False):
    total = None
    for slot in range(slots):
        matrix = mats[at + slot]
        part = expand(lists, slot, rows, matrix, cols)
        part = jnp.where(lists.same(slot, rows, cols), part, 0.0)
        total = part if total is None else total + part
    return total


def store_split(high_ref, low_ref, rows, cols, value):
    high, low = split(value)
    high_ref[pl.ds(*rows), pl.ds(*cols)] = high
    low_ref[pl.ds(*rows), pl.ds(*cols)] = low


def lanes_of(shape):
    return lax.broadcasted_iota(jnp.int32, shape, 1)


def keep(value, low, high):
    lane = lanes_of(value.shape)
    return jnp.where((lane >= low) & (lane < high), value, 0.0)


def moved_to(value, source, target, count):
    shift = (target - source) % 128
    if shift:
        value = pltpu.roll(value, shift, 1)
    return keep(value, target, target + count)


def wide_from_items(value, source, target):
    head = moved_to(value, source, target, 49)
    tail = moved_to(value[0:128], source + 49, target, 25) + moved_to(
        value[128:256], source + 49, target + 25, 24
    )
    return jnp.concatenate([head, tail], axis=0)


def items_from_wide(value):
    head = keep(value[0:256], 0, 49)
    tail = value[256:384]
    low = moved_to(tail, 0, 49, 25)
    high = moved_to(tail, 25, 49, 24)
    return head + jnp.concatenate([low, high], axis=0)


def narrow_from_items(value, source, target):
    return moved_to(value[0:128], source, target, 13) + moved_to(
        value[128:256], source, target + 13, 12
    )


def items_from_narrow(value):
    return jnp.concatenate([moved_to(value, 0, 110, 13), moved_to(value, 13, 110, 12)], axis=0)


def items_of(sums):
    left = items_from_wide(taller(sums["e"], 384)) + moved_to(taller(sums["one"], 256), 0, 74, 36)
    right = (
        items_from_wide(taller(sums["o"], 384))
        + moved_to(taller(sums["two"], 256), 0, 74, 36)
        + items_from_narrow(sums["three"])
    )
    return left, right


def own_views(own_ref):
    left, right = received_blocks(own_ref)
    return (
        wide_from_items(left, 0, 0),
        wide_from_items(right, 0, 0),
        moved_to(left, 74, 0, 36),
        moved_to(right, 74, 0, 36),
        narrow_from_items(right, 110, 0),
    )


row_units = (
    [((1, 2), mode) for mode in (5, 6, 7)]
    + [((0,), mode) for mode in (5, 6, 7)]
    + [((3,), mode) for mode in (5, 6, 7)]
    + [((state,), mode) for state in range(4) for mode in (3, 4)]
)
col_units = [(states, mode) for states in ((1, 2), (0,), (3,)) for mode in (0, 1, 2)]


def density_tables():
    def entries(units, second):
        listed = []
        for unit, (states, mode) in enumerate(units):
            for half, state in enumerate(states):
                width = widths[state]
                for low in range(width):
                    for high in range(low, width):
                        shift = high - low
                        place = shift * 8 + low if shift <= 4 else (8 - shift) * 8 + high
                        listed.append((second * half + 40 * unit + place, state, mode, low, high))
        return listed

    pick = np.zeros((512, 1024), np.float32)
    rows = np.zeros((64, 2, 2048), np.float32)
    cols = np.zeros((2, 2048, 128), np.float32)

    def place_entry(at, state, mode, low, high):
        rows[mode * 8 + low, 0, at] = 1.0
        cols[0, at, state * 8 + high] = 1.0
        if low != high:
            rows[mode * 8 + high, 1, at] = 1.0
            cols[1, at, state * 8 + low] = 1.0
        elif state == 0 and mode in (0, 1, 3):
            cols[1, at, 6] = 1.0
            if mode == 3:
                rows[6, 1, at] = rows[14, 1, at] = 1.0
            else:
                rows[mode * 8 + 6, 1, at] = -1.0

    for entry in entries(row_units, 768):
        place_entry(*entry)
    lanes = iter(
        128 * block + lane for block, span in enumerate(spare_lanes) for lane in range(*span)
    )
    for at, state, mode, low, high in entries(col_units, 384):
        if state == 0 and mode < 2 and low == 6:
            continue
        lane = next(lanes)
        pick[at, lane] = 1.0
        place_entry(1024 + lane, state, mode, low, high)
    rows = rows.reshape(64, 4096)
    cols = cols.reshape(4, 1024, 128)[:, :, 0:32].transpose(1, 0, 2).reshape(1024, 128)
    return [jnp.asarray(value.astype(bf16)) for value in (pick, rows, cols)]


def shifted_sums(loads):
    sums = [None] * 5
    for value in loads:
        for shift in range(5):
            other = pltpu.roll(value, 8 - shift, 0) if shift else value
            part = value * other
            sums[shift] = part if sums[shift] is None else sums[shift] + part
    return sums


def three_mode_loads(ref, slot, width):
    step = width ** (2 - slot)
    lead = [0] if slot == 0 else [at * step * width for at in range(width**slot)]
    for first in lead:
        for inner in range(step):
            yield ref[pl.ds(first + inner, 8, stride=step), :]


def two_mode_loads(ref, lanes, start, slot, width):
    for inner in range(width):
        for low in lanes:
            if slot == 0:
                yield ref[low, pl.ds(start + inner, 8, stride=width), :]
            else:
                yield ref[low, pl.ds(start + inner * width, 8), :]


def lane_totals(parts, padded):
    if len(parts) * 8 < padded:
        parts = parts + [jnp.zeros((padded - 8 * len(parts), 128), f32)]
    stacked = split(jnp.concatenate(parts, axis=0))
    row = lax.broadcasted_iota(jnp.int32, (8, 128), 0)
    lane = lanes_of((8, 128))
    wanted = (row == 0) | ((row == 1) & (lane < 64)) | ((row == 2) & (lane >= 64))
    select = jnp.where(wanted, 1.0, 0.0).astype(bf16)
    totals = mm_nt(select, stacked[0]) + mm_nt(select, stacked[1])
    lane = lanes_of((1, padded))
    return jnp.where(lane < 120, totals[1:2], totals[0:1]), totals[2:3]


def pack_kernel(
    zero_ref, one_ref, two_ref, three_ref, send_ref, items, tails, last, wide, middle, narrow
):
    items[...] = jnp.zeros((2, 256, 128), f32)
    tails[...] = jnp.zeros((1, 128, 128), f32)
    last[...] = jnp.zeros((1, 40, 128), f32)
    for lead in range(49):
        for row in range(2):
            start = 343 * lead
            at = 128 * row + lead
            half, place = divmod(lead, 25)
            place += 128 * row + 49
            for block in range(2):
                items[block, at : at + 1, :] = zero_ref[
                    row : row + 1, start + 128 * block : start + 128 * block + 128
                ]
            tail = zero_ref[row : row + 1, start + 256 : start + 343]
            items[half, place : place + 1, 0:87] = tail
            tails[0, 64 * row + lead : 64 * row + lead + 1, 0:87] = tail
    for lead in range(36):
        for ref, at in ((one_ref, 74 + lead), (two_ref, 202 + lead)):
            start = 216 * lead
            items[0, at : at + 1, :] = ref[0:1, start : start + 128]
            items[1, at : at + 1, 0:88] = ref[0:1, start + 128 : start + 216]
    for lead in range(25):
        half, place = divmod(lead, 13)
        value = three_ref[0:1, 125 * lead : 125 * lead + 125]
        items[half, 238 + place : 239 + place, 0:125] = value
        last[0, lead : lead + 1, 0:125] = value

    def turned(start):
        return jnp.concatenate([items[0, start : start + 128, :].T, items[1, start : start + 128, :].T])

    left, right = turned(0), turned(128)
    wide[0:384, :] = wide_from_items(left, 0, 0) + wide_from_items(right, 0, 64)
    wide[384:392, :] = jnp.zeros((8, 128), f32)
    middle[0:256, :] = moved_to(left, 74, 0, 36) + moved_to(right, 74, 64, 36)
    middle[256:288, :] = jnp.zeros((32, 128), f32)
    narrow[0:128, :] = narrow_from_items(right, 110, 0)
    narrow[128:200, :] = jnp.zeros((72, 128), f32)
    parts = []
    for ref, width in ((middle, 6), (wide, 7), (narrow, 5)):
        for slot in range(3):
            parts += shifted_sums(three_mode_loads(ref, slot, width))
    for slot in range(2):
        parts += shifted_sums(
            itertools.chain(
                two_mode_loads(items, (0, 1), 0, slot, 7),
                two_mode_loads(items, (0, 1), 128, slot, 7),
                two_mode_loads(tails, (0,), 0, slot, 7),
                two_mode_loads(tails, (0,), 64, slot, 7),
            )
        )
    for start in (74, 202):
        for slot in range(2):
            parts += shifted_sums(two_mode_loads(items, (0, 1), start, slot, 6))
    for slot in range(2):
        parts += shifted_sums(two_mode_loads(last, (0,), 0, slot, 5))
    first, second = lane_totals(parts, 768)
    for at in range(3):
        for block in range(2):
            low = 256 * at + 128 * block
            items[block, 110 + at : 111 + at, :] = first[:, low : low + 128]
    for block in range(2):
        items[block, 113:114, :] = second[:, 128 * block : 128 * block + 128]
    left = turned(0)
    send_ref[:, 0, 0:128] = left
    send_ref[:, 0, 128:256] = right


def lead_kernel(
    row_ref,
    col_ref,
    pair_ref,
    mode_ref,
    strength_ref,
    over_ref,
    pos_ref,
    intra_zero,
    intra_one,
    intra_two,
    intra_three,
    order_ref,
    *rest,
):
    out_refs, held, (mats, weights, sems) = rest[0:6], rest[6:12], rest[12:]
    la_high, la_low, lb_high, lb_low, lc_high, lc_low = held
    copies = [
        pltpu.make_async_copy(held[at], out_refs[at], sems.at[at]) for at in range(6)
    ]
    lists = Lists(row_ref, col_ref)
    fill_weights(pair_ref, mode_ref, strength_ref, weights)
    both = [(pair, flipped, range(3)) for pair in range(3) for flipped in (False, True)]
    fill_coupling(mats, over_ref, pos_ref, weights, both)
    fill_operators(mats, (intra_zero, intra_one, intra_two, intra_three), range(3))
    la = functools.partial(store_split, la_high, la_low)
    lb = functools.partial(store_split, lb_high, lb_low)
    lc = functools.partial(store_split, lc_high, lc_low)
    even, odd, one, three = ((list_at[name][0], 224) for name in ("e", "o", "r1", "r3"))
    from_zero, from_one, from_three = (list_at[name] for name in ("b0", "r1", "b3"))

    def kron(pair, rows, cols, flipped):
        return kron_three(lists, mats, pair, (0, 1, 2), rows, cols, flipped)

    def own(state, rows, cols):
        return sum_slots(lists, mats, 96 + 8 * state, 3, rows, cols)

    def tile(store, row, col, value):
        store((row, value.shape[0]), (col, value.shape[1]), value)

    zero_part, one_part = kron(0, one, from_zero, True)
    tile(la, 0, 0, zero_part)
    tile(la, 224, 0, one_part)
    zero_part, one_part = kron(2, three, from_one, True)
    tile(la, 0, 384, zero_part)
    tile(la, 224, 384, one_part)
    zero_part, one_part = kron(2, one, from_three, False)
    tile(la, 0, 640, zero_part)
    tile(la, 224, 640, one_part)
    tile(la, 448, 0, own(0, odd, from_zero))
    tile(la, 448, 384, own(2, one, from_one))
    tile(la, 448, 640, own(3, three, from_three))
    copies[0].start()
    copies[1].start()
    tile(lb, 0, 0, own(0, even, from_zero))
    tile(lb, 0, 384, own(1, one, from_one))
    zero_part, one_part = kron(0, (even[0], 176), from_one, False)
    tile(lc, 0, 0, zero_part)
    tile(lc, 0, 256, one_part)
    zero_part, one_part = kron(0, odd, from_one, False)
    tile(lc, 0, 512, zero_part[0:176])
    tile(lc, 176, 512, one_part)
    zero_part, one_part = kron(1, one, from_one, True)
    tile(lc, 176, 0, zero_part)
    tile(lc, 176, 256, one_part)
    copies[4].start()
    copies[5].start()
    zero_part, one_part = kron(1, one, from_one, False)
    tile(lb, 0, 640, zero_part)
    tile(lb, 0, 896, one_part)
    copies[2].start()
    copies[3].start()
    for copy in copies:
        copy.wait()


def received_blocks(recv_ref):
    return recv_ref[:, 0, 0:128], recv_ref[:, 0, 128:256]


def middle_kernel(recv_ref, pick_ref, *rest):
    in_refs, send_ref, held = rest[0:6], rest[6], rest[7:13]
    wide, middle, narrow, pick_held, sems = rest[13:]
    picking = pltpu.make_async_copy(pick_ref, pick_held, sems.at[6])
    picking.start()
    copies = [pltpu.make_async_copy(in_refs[at], held[at], sems.at[at]) for at in range(6)]
    for copy in copies:
        copy.start()
    left, right = received_blocks(recv_ref)
    wide[pl.ds(0, 172, stride=2), :] = keep(left[0:172], 0, 74)
    wide[pl.ds(1, 172, stride=2), :] = keep(right[0:172], 0, 74)
    wide[344:392, :] = jnp.zeros((48, 128), f32)
    middle[0:256, :] = moved_to(left, 74, 0, 36) + moved_to(right, 74, 64, 36)
    middle[256:288, :] = jnp.zeros((32, 128), f32)
    narrow[...] = keep(right[0:200], 110, 123)
    parts = []
    for ref, width in ((middle, 6), (wide, 7), (narrow, 5)):
        for slot in range(3):
            parts += shifted_sums(three_mode_loads(ref, slot, width))
    first, second = lane_totals(parts, 384)
    entries = split(jnp.concatenate([first, second[:, 0:128]], axis=1))
    picking.wait()
    picked = mm(entries[0], pick_held[...]) + mm(entries[1], pick_held[...])
    summed = moved_to(jnp.sum(left, axis=0, keepdims=True), 110, 72, 4)

    def put(block, value):
        span = slice(128 * block, 128 * block + 128)
        extra = picked[:, span]
        if block == 6:
            extra = extra + summed
        rows = value.shape[0]
        send_ref[0:rows, 0, span] = value + extra
        send_ref[rows:256, 0, span] = jnp.broadcast_to(extra, (256 - rows, 128))

    from_zero = split(wide[0:384, :])
    one_at = [split(moved_to(left, 74, target, 36)) for target in (74, 0, 36, 72)]
    two_at = [split(moved_to(right, 74, target, 36)) for target in (74, 0, 36)]
    from_three = split(keep(right[0:128], 110, 123))

    def product(at, stack, cols=slice(None)):
        high = jnp.concatenate([part[0] for part in stack], axis=0)
        low = jnp.concatenate([part[1] for part in stack], axis=0)
        return mm_wide((held[at][:, cols], held[at + 1][:, cols]), (high, low))

    for copy in copies:
        copy.wait()
    value = product(0, [from_zero, two_at[0], from_three])
    put(0, value[0:224])
    put(1, value[224:448])
    put(3, value[448:672])
    put(2, product(2, [from_zero, one_at[0]], slice(0, 640)))
    value = product(4, one_at[1:])
    put(4, value[0:176])
    put(5, value[176:400])
    put(6, product(2, two_at[1:], slice(640, 1152)))
    send_ref[:, 0, 896:1024] = jnp.broadcast_to(picked[:, 896:1024], (256, 128))


directions = (
    (0, False, "b0", "b1", "p6", "t7"),
    (0, True, "b1", "b0", "p7", "t6"),
    (1, False, "b1", "b1", "p6", "t6"),
    (1, True, "b1", "b1", "p6", "t6"),
    (2, False, "b1", "b3", "p5", "t6"),
    (2, True, "b3", "b1", "p6", "t5"),
)


homes = ((0, "b0", "t7"), (1, "b1", "t6"), (2, "b1", "t6"), (3, "b3", "t5"))


def tail_kernel(
    row_ref,
    col_ref,
    lane_ref,
    lcol_ref,
    pair_ref,
    mode_ref,
    strength_ref,
    over_ref,
    pos_ref,
    intra_zero,
    intra_one,
    intra_two,
    intra_three,
    own_ref,
    order_ref,
    *rest,
):
    outs, (mats, weights) = rest[:-2], rest[-2:]
    lists, lanes = Lists(row_ref, col_ref), Lists(lane_ref, lcol_ref)
    fill_weights(pair_ref, mode_ref, strength_ref, weights)
    wanted = []
    for pair, flipped, *_ in directions:
        wanted += [(pair, flipped, (5, 6, 7)), (pair, not flipped, (3, 4))]
    fill_coupling(mats, over_ref, pos_ref, weights, wanted)
    row = lax.broadcasted_iota(jnp.int32, (128, 128), 0)
    for at, (pair, flipped, target, source, from_lanes, to_lanes) in enumerate(directions):
        three_high, three_low, two_ref = outs[3 * at : 3 * at + 3]
        rows, cols = (list_at[target][0], target_rows[target]), list_at[source]
        over, moved = kron_three(lists, mats, pair, (5, 6, 7), rows, cols, flipped)
        store_split(three_high, three_low, (0, rows[1]), (0, cols[1]), over)
        store_split(three_high, three_low, (rows[1], rows[1]), (0, cols[1]), moved)
        lanes_in = (128 * lane_kinds[from_lanes], 128)
        lanes_out = (128 * lane_kinds[to_lanes], 128)
        base = pair * 32 + (0 if flipped else 16) + 3

        def factor(slot, extra):
            return expand(lanes, slot, lanes_in, mats[base + extra + slot], lanes_out)

        first, second = factor(0, 0), factor(1, 0)
        over = first * second
        moved = factor(0, 8) * second + first * factor(1, 8)
        upper, lower = split(jnp.where(row < 64, moved, over)), split(jnp.where(row < 64, over, 0.0))
        for part in range(2):
            two_ref[0:128, 128 * part : 128 * part + 128] = upper[part]
            two_ref[128:256, 128 * part : 128 * part + 128] = lower[part]
    base_ref = outs[-1]
    sums = {}
    for state, ref in enumerate((intra_zero, intra_one, intra_two, intra_three)):
        for mode in range(3, 8):
            value = ref[:, mode, :]
            put_matrix(mats, 96 + 8 * state + mode, value.T if mode < 5 else value)
    views = own_views(own_ref)
    for state, index, kind in homes:
        rows, cols = (list_at[index][0], target_rows[index]), list_at[index]
        span = (128 * lane_kinds[kind], 128)
        three = split(sum_slots(lists, mats, 96 + 8 * state + 5, 3, rows, cols))
        two = split(sum_slots(lanes, mats, 96 + 8 * state + 3, 2, span, span))
        used = views[0:2] if state == 0 else views[state + 1 : state + 2]
        names = ("e", "o") if state == 0 else (("one", "two", "three")[state - 1],)
        for view, name in zip(used, names):
            sums[name] = mm_wide(three, split(view)) + mm_wide(split(view[0 : rows[1]]), two)
    left, right = items_of(sums)
    own_left, own_right = received_blocks(own_ref)
    base_ref[:, 0:128] = own_left - time_step * left
    base_ref[:, 128:256] = own_right - time_step * right


def last_kernel(back_ref, *rest):
    count = 21
    in_refs, rest = rest[:count], rest[count:]
    zero_ref, one_ref, two_ref, three_ref, *density_refs = rest[:8]
    items, *held, sems = rest[8:]
    copies = [pltpu.make_async_copy(in_refs[at], held[at], sems.at[at]) for at in range(count)]
    for at in (19, 20, *range(19)):
        copies[at].start()
    base_ref, rows_ref, cols_ref = held[18:21]

    def block(at):
        return back_ref[:, 0, 128 * at : 128 * at + 128]

    first, second, fifth, sixth, seventh = (block(at) for at in (0, 1, 4, 5, 6))
    copies[19].wait()
    copies[20].wait()
    totals = []
    for at, span in enumerate(spare_lanes):
        totals.append(keep(jnp.sum(block(at), axis=0, keepdims=True), *span))
    total = jnp.concatenate(totals, axis=1)
    turned = seventh.T
    entries = jnp.concatenate([turned[72 + at : 73 + at, :] for at in range(4)] + [total], axis=1)
    quarters = []
    for quarter in range(4):
        part = entries[:, 1024 * (quarter % 2) : 1024 * (quarter % 2) + 1024]
        quarters.append(rows_ref[:, 1024 * quarter : 1024 * quarter + 1024].astype(f32) * part)
    high, low = split(jnp.concatenate(quarters, axis=0))
    placed = mm(high, cols_ref[...]) + mm(low, cols_ref[...])
    density = placed[0:64]
    for quarter in range(1, 4):
        density += pltpu.roll(placed[64 * quarter : 64 * quarter + 64], 128 - 32 * quarter, 1)
    for state, ref in enumerate(density_refs):
        width = widths[state]
        value = density * (1.0 / float(width**7))
        for mode in range(8):
            ref[:, mode, :] = value[mode * 8 : mode * 8 + width, state * 8 : state * 8 + width]

    even_in = moved_to(fifth, 0, 0, 36) + moved_to(fifth, 36, 64, 36)
    odd_in = moved_to(fifth, 72, 0, 36) + moved_to(sixth, 72, 64, 36)
    inputs = (
        jnp.concatenate([even_in, odd_in], axis=1),
        wide_from_items(first, 0, 0) + wide_from_items(second, 0, 64),
        moved_to(seventh, 0, 0, 36) + moved_to(seventh, 36, 64, 36),
        moved_to(sixth, 0, 0, 36) + moved_to(sixth, 36, 64, 36),
        narrow_from_items(first, 110, 0) + narrow_from_items(second, 110, 64),
        moved_to(first, 74, 0, 36) + moved_to(second, 74, 64, 36),
    )
    for copy in copies[0:19]:
        copy.wait()
    sums = {}
    targets = (("e", "o"), ("one",), ("one",), ("two",), ("two",), ("three",))
    for at, value in enumerate(inputs):
        three_high, three_low, two = held[3 * at : 3 * at + 3]
        height = three_high.shape[0] // 2
        product = mm_wide if value.shape[1] == 128 else mm3
        middle = product((three_high[...], three_low[...]), split(value))
        for which, name in enumerate(targets[at]):
            lanes = slice(128 * which, 128 * which + 128)
            both = split(jnp.concatenate([middle[0:height, lanes], middle[height:, lanes]], axis=1))
            part = mm(both[0], two[...])
            part = part[:, 0:128] + part[:, 128:256] + mm(both[1], two[:, 0:128])
            sums[name] = part if name not in sums else sums[name] + part
    left, right = items_of(sums)
    items[0:128, :] = (base_ref[:, 0:128] - time_step * (left + block(2))).T
    items[128:256, :] = (base_ref[:, 128:256] - time_step * (right + block(3))).T
    for lead in range(49):
        for row in range(2):
            start = 343 * lead
            at = 128 * row
            zero_ref[row : row + 1, start : start + 256] = items[at + lead : at + lead + 1, 0:256]
            place, half = (lead, 0) if lead < 25 else (lead - 25, 128)
            zero_ref[row : row + 1, start + 256 : start + 343] = items[
                at + 49 + place : at + 50 + place, half : half + 87
            ]
    for lead in range(36):
        start = 216 * lead
        one_ref[0:1, start : start + 216] = items[74 + lead : 75 + lead, 0:216]
        two_ref[0:1, start : start + 216] = items[202 + lead : 203 + lead, 0:216]
    for lead in range(25):
        start = 125 * lead
        place, half = (lead, 0) if lead < 13 else (lead - 13, 128)
        three_ref[0:1, start : start + 125] = items[238 + place : 239 + place, half : half + 125]


def local(*args):
    states = args[:4]
    intra = [jnp.transpose(value, (1, 0, 2)) for value in args[4:8]]
    over, pos = (jnp.transpose(value, (0, 2, 1, 3)) for value in args[8:10])
    pair, mode, strength = args[10:]
    tables = [jnp.asarray(table) for table in digit_tables()]
    pick, density_rows, density_cols = density_tables()
    vm = pl.BlockSpec(memory_space=pltpu.VMEM)
    sm = pl.BlockSpec(memory_space=pltpu.SMEM)
    hbm = pl.BlockSpec(memory_space=pl.ANY)

    def call(kernel, operands, outs, scratch=(), specs=None, out_specs=None, megabytes=56):
        return pl.pallas_call(
            kernel,
            out_shape=[jax.ShapeDtypeStruct(shape, kind) for shape, kind in outs],
            in_specs=specs or [vm] * len(operands),
            out_specs=out_specs or [vm] * len(outs),
            scratch_shapes=list(scratch),
            compiler_params=pltpu.CompilerParams(vmem_limit_bytes=int(megabytes * 1024 * 1024)),
        )(*operands)

    def exchange(value):
        return lax.all_to_all(value, axes, split_axis=0, concat_axis=0, tiled=True)

    column = [pltpu.VMEM((392, 128), f32), pltpu.VMEM((288, 128), f32), pltpu.VMEM((200, 128), f32)]
    with jax.named_scope("pack"):
        (send,) = call(
            pack_kernel,
            states,
            [((256, 1, 256), f32)],
            [
                pltpu.VMEM((2, 256, 128), f32),
                pltpu.VMEM((1, 128, 128), f32),
                pltpu.VMEM((1, 40, 128), f32),
                *column,
            ],
        )
    with jax.named_scope("forward"):
        recv = exchange(send)
    mats = [pltpu.VMEM((mats_count, 24, 8), f32), pltpu.SMEM((24,), f32)]
    held = [pltpu.VMEM(shape, bf16) for shape in lead_shapes]
    with jax.named_scope("lead_matrices"):
        lead = call(
            lead_kernel,
            [*tables[:2], pair, mode, strength, over, pos, *intra, send],
            [(shape, bf16) for shape in lead_shapes],
            [*held, *mats, pltpu.SemaphoreType.DMA((6,))],
            [vm] * 2 + [sm] * 3 + [vm] * 6 + [hbm],
            [hbm] * 6,
        )
    with jax.named_scope("lead_products"):
        (outgoing,) = call(
            middle_kernel,
            [recv, pick, *lead],
            [((256, 1, 1024), f32)],
            [*held, *column, pltpu.VMEM(pick.shape, bf16), pltpu.SemaphoreType.DMA((7,))],
            [vm] + [hbm] * 7,
            megabytes=53.4,
        )
    with jax.named_scope("back"):
        back = exchange(outgoing)
    with jax.named_scope("tail_matrices"):
        tail_outs = []
        for pair_at, flipped, target, source, from_lanes, to_lanes in directions:
            tail_outs += [((2 * target_rows[target], list_at[source][1]), bf16)] * 2
            tail_outs.append(((256, 256), bf16))
        tail_outs.append(((256, 256), f32))
        tails = call(
            tail_kernel,
            [*tables, pair, mode, strength, over, pos, *intra, send, outgoing],
            tail_outs,
            mats,
            [vm] * 4 + [sm] * 3 + [vm] * 7 + [hbm],
        )
    with jax.named_scope("tail_products"):
        late = [*tails, density_rows, density_cols]
        outs = call(
            last_kernel,
            [back, *late],
            [(state.shape, f32) for state in states]
            + [((width, 8, width), f32) for width in widths],
            [
                pltpu.VMEM((256, 256), f32),
                *[pltpu.VMEM(value.shape, value.dtype) for value in late],
                pltpu.SemaphoreType.DMA((len(late),)),
            ],
            [vm] + [hbm] * len(late),
        )
    densities = [jnp.transpose(value, (1, 0, 2)) for value in outs[4:]]
    return (*outs[:4], *densities)


def solution(mesh):
    rows = P(axes, None)
    in_specs = (rows,) * 4 + (P(),) * 9
    out_specs = (rows,) * 4 + (P(),) * 4
    return jax.shard_map(local, mesh=mesh, in_specs=in_specs, out_specs=out_specs, check_vma=False)
```
